256 devices in a mesh: site: 8 (over z), sector: 32 (over x, y, core).
Axes of the slice: x: 4, y: 4, z: 8, core: 2. Of those that a mesh axis runs over, the one named last changes fastest.
Arguments:
- initial_state: float32 [8, 32, 128, 128], P('site', 'sector')
- left_env: bfloat16 [8, 32, 4, 12, 128, 128], P('site', 'sector'), may hold values from -0.5 to 0.5
- edge_env: bfloat16 [32, 4, 12, 128, 128], P('sector'), may hold values from -0.5 to 0.5
- right_env: bfloat16 [8, 32, 4, 12, 128, 128], P('site', 'sector'), may hold values from -0.15625 to 0.15625
- source_blocks: int32 [8, 32, 4], P('site', 'sector'), may hold values from 0 to 31, as said below
- live_terms: int32 [8, 32], P('site', 'sector'), may hold values from 1 to 4
Outputs:
- state: float32 [8, 32, 128, 128], P('site', 'sector')
- energy: float32 [8], P('site')
The draws below stay inside these ranges and needn't reach their ends.
Inputs may be any that keep to these rules, and one draw needn't show every extreme that they name: source_blocks[s, b, 0] = b; every other entry is b - 1, b + 1, b - 4 or b + 4.
All inputs are finite; a program needn't handle non-finite values.
Results may differ from the reference program's by a relative error of at most 0.015.
Values may be sent and summed in bfloat16 or wider, within the bound.
A program may use at most 64 MiB of HBM per device.

```python
import math
import jax
import jax.numpy as jnp
from jax import lax

M = 128
TERMS = 12
NSRC = 4
GRID = 4
ITERS = 8
NB = 32
SEGS = 8


def draw_initial_state(key, part):
    key = jax.random.fold_in(key, 1)
    shape = (SEGS, NB, M, M)
    block = jax.lax.broadcasted_iota(jnp.float32, shape, 1)
    scale = jnp.exp(math.log(3.0) * block / (NB - 1))
    values = jax.random.normal(key, shape, jnp.float32)
    return (values * scale).astype(jnp.float32)


def draw_source_blocks(key, part):
    key = jax.random.fold_in(key, 2)
    shape = (SEGS, NB, NSRC)
    block = jax.lax.broadcasted_iota(jnp.int32, shape, 1)
    column = jax.lax.broadcasted_iota(jnp.int32, shape, 2)
    picked = jax.random.randint(key, shape, 0, 4)
    offset = jnp.where(picked == 0, -1, jnp.where(picked == 1, 1, jnp.where(picked == 2, -GRID, GRID)))
    target = block + offset
    outside = (target < 0) | (target >= NB)
    target = jnp.where(outside, block - offset, target)
    target = jnp.where(column == 0, block, target)
    return target.astype(jnp.int32)


def draw_live_terms(key, part):
    key = jax.random.fold_in(key, 3)
    first_key, second_key = jax.random.split(key)
    counts = jax.random.randint(first_key, (SEGS, NB), 1, NSRC + 1)
    position = jax.random.randint(second_key, (SEGS, 1), 0, NB)
    block = jax.lax.broadcasted_iota(jnp.int32, (SEGS, NB), 1)
    counts = jnp.where(block == position, NSRC, counts)
    counts = jnp.where(block == (position + 1) % NB, 1, counts)
    return counts.astype(jnp.int32)


def steps_of(stream_key, extent, shards, smallest, high):
    gain, own = 1.0, jax.random.fold_in(stream_key, 6)
    for axis_at, shards_of in shards:
        steps = jnp.exp(jax.random.uniform(jax.random.fold_in(own, axis_at), (shards_of,), jnp.float32, smallest / len(shards), high / len(shards)))
        gain = gain * jnp.repeat(steps, extent[axis_at] // shards_of).reshape([-1 if axis == axis_at else 1 for axis in range(len(extent))])
    return gain


def gaussian(own_key, shape, deviation, limit, shards=(), held_as=jnp.bfloat16):
    loudness = steps_of(own_key, shape, shards, -0.22, 0.18) if shards else 1.0
    drawn = jax.random.normal(own_key, shape, jnp.float32) * deviation * loudness
    return jnp.minimum(jnp.maximum(drawn, -limit), limit).astype(held_as)


def setup_inputs(seed: int = 0) -> dict:
    splits = jax.random.split(jax.random.key(seed), 7)
    return {
        "initial_state": draw_initial_state(jax.random.fold_in(splits[6], 71), 0),
        "left_env": gaussian(splits[1], (SEGS, NB, NSRC, TERMS, M, M), M ** -0.5, 0.5, ((0, 8), (1, 32))),
        "edge_env": gaussian(splits[2], (NB, NSRC, TERMS, M, M), M ** -0.5, 0.5, ((0, 32),)),
        "right_env": gaussian(splits[3], (SEGS, NB, NSRC, TERMS, M, M), (M * TERMS) ** -0.5, 0.15625, ((0, 8), (1, 32))),
        "source_blocks": draw_source_blocks(jax.random.fold_in(splits[6], 71), 0),
        "live_terms": draw_live_terms(jax.random.fold_in(splits[6], 71), 0),
    }


def apply_hamiltonian(vector, left_side, right_side, source_ids, live_count):
    rounded = vector.astype(jnp.bfloat16)

    def one_block(packed):
        left_block, right_block, sources, count = packed
        total = jnp.zeros((M, M), jnp.float32)
        for j in range(NSRC):
            piece = lax.dynamic_index_in_dim(rounded, sources[j].astype(jnp.int32), 0, keepdims=False)
            product = jnp.einsum('wlk,kr->wlr', left_block[j].astype(jnp.float32), piece.astype(jnp.float32))
            product = product.astype(jnp.bfloat16)
            term = jnp.einsum('wls,wsr->lr', product.astype(jnp.float32), right_block[j].astype(jnp.float32))
            total = total + jnp.where(j < count, term, jnp.float32(0.0))
        return total
    return lax.map(one_block, (left_side, right_side, source_ids, live_count))

def mean_inner(first, second):
    return jnp.sum(first * second) / (NB * M * M)

def segment_solve(start_state, left_side, right_side, source_ids, live_count):

    def operate(vector):
        return apply_hamiltonian(vector, left_side, right_side, source_ids, live_count)
    wave_now = start_state / jnp.sqrt(mean_inner(start_state, start_state) + 1e-06)
    wave_image = operate(wave_now)
    energy = jnp.float32(0.0)
    for step in range(ITERS):
        rayleigh = mean_inner(wave_now, wave_image)
        residual = wave_image - rayleigh * wave_now
        resid_norm = mean_inner(residual, residual)
        correction = residual / jnp.sqrt(resid_norm + 1e-06)
        corr_image = operate(correction)
        off_diag = 0.5 * (mean_inner(correction, wave_image) + mean_inner(wave_now, corr_image))
        corr_energy = mean_inner(correction, corr_image)
        half_gap = 0.5 * (rayleigh - corr_energy)
        rotation = 0.5 * jnp.arctan2(-off_diag, -half_gap)
        energy = 0.5 * (rayleigh + corr_energy) - jnp.sqrt(half_gap * half_gap + off_diag * off_diag)
        cosine = jnp.cos(rotation)
        sine = jnp.sin(rotation)
        wave_now = cosine * wave_now + sine * correction
        wave_image = cosine * wave_image + sine * corr_image
    return (wave_now, energy)

def reference(initial_state, left_env, edge_env, right_env, source_blocks, live_terms):
    states = []
    energies = []
    for s in range(SEGS):
        left_side = edge_env if s == 0 else left_env[s - 1]
        wave_now, energy = segment_solve(initial_state[s], left_side, right_env[s], source_blocks[s], live_terms[s])
        states.append(wave_now)
        energies.append(energy)
    return (jnp.stack(states), jnp.stack(energies))
```

```python
import functools

import jax
import jax.numpy as jnp
from jax import lax
from jax.experimental import pallas as pl
from jax.experimental.pallas import tpu as pltpu
from jax.sharding import PartitionSpec as P

GRID = 4
ITERS = 8
GROUP = 3
HALO = jnp.bfloat16
EPS = 1e-06
MESH = pl.DeviceIdType.MESH
F32 = jnp.float32
BF16 = jnp.bfloat16


def kernel(
    blocks, cells, sites, nsrc, terms,
    start_ref, left_ref, edge_ref, right_ref, ids_ref, live_ref,
    state_ref, energy_ref,
    env, renv, xs, ys, ts, zown, start_halo, zsend, zhalo_even, zhalo_odd, row_send, rows,
    env_send, env_recv, renv_sem, start_send, start_recv,
    halo_send, halo_recv, row_send_sem, row_recv_sem,
):
    site = lax.axis_index("site")
    me = lax.axis_index("sector")
    width = start_ref.shape[-1]
    steps = [(p, g) for p in range(nsrc // 2) for g in range(terms // GROUP)]

    def peer(by):
        return lax.rem(me + by + blocks, blocks)

    barrier = pltpu.get_barrier_semaphore()

    @pl.when(site > 0)
    def _():
        pl.semaphore_signal(barrier, inc=1, device_id={"site": site - 1}, device_id_type=MESH)

    @pl.when(site < sites - 1)
    def _():
        pl.semaphore_signal(barrier, inc=1, device_id={"site": site + 1}, device_id_type=MESH)

    for d in range(1, blocks):
        pl.semaphore_signal(barrier, inc=1, device_id={"sector": peer(d)}, device_id_type=MESH)

    def span(ref, p, g):
        return ref.at[pl.ds(2 * p, 2), pl.ds(g * GROUP * width, GROUP * width), :]

    for i, (p, g) in enumerate(steps):
        pltpu.make_async_copy(span(right_ref, p, g), span(renv, p, g), renv_sem.at[i]).start()

    @pl.when(site == 0)
    def _():
        for i, (p, g) in enumerate(steps):
            pltpu.make_async_copy(span(edge_ref, p, g), span(env, p, g), env_recv.at[i]).start()

    pl.semaphore_wait(
        barrier, blocks - 1 + jnp.where(site > 0, 1, 0) + jnp.where(site < sites - 1, 1, 0)
    )

    def env_copy(i, p, g):
        return pltpu.make_async_remote_copy(
            src_ref=span(left_ref, p, g), dst_ref=span(env, p, g),
            send_sem=env_send.at[i], recv_sem=env_recv.at[i],
            device_id={"site": site + 1}, device_id_type=MESH,
        )

    @pl.when(site < sites - 1)
    def _():
        for i, (p, g) in enumerate(steps):
            env_copy(i, p, g).start()

    hops = (1, -1, GRID, -GRID)
    zhalo = (zhalo_even, zhalo_odd)

    def start_copy(n):
        return pltpu.make_async_remote_copy(
            src_ref=start_ref, dst_ref=start_halo.at[n],
            send_sem=start_send.at[n], recv_sem=start_recv.at[n],
            device_id={"sector": peer(hops[n])}, device_id_type=MESH,
        )

    def halo_copy(n, slot):
        return pltpu.make_async_remote_copy(
            src_ref=zsend.at[slot], dst_ref=zhalo[slot].at[n],
            send_sem=halo_send.at[slot, n], recv_sem=halo_recv.at[slot, n],
            device_id={"sector": peer(hops[n])}, device_id_type=MESH,
        )

    def send_rows(values, slot):
        lane = lax.broadcasted_iota(jnp.int32, (1, width), 1)
        row = jnp.zeros((1, width), F32)
        for n, value in enumerate(values):
            row = jnp.where(lane == n, value, row)
        row_send[slot] = row
        rows[slot, me] = row
        for d in range(1, blocks):
            pltpu.make_async_remote_copy(
                src_ref=row_send.at[slot], dst_ref=rows.at[slot, me],
                send_sem=row_send_sem.at[slot], recv_sem=row_recv_sem.at[slot],
                device_id={"sector": peer(d)}, device_id_type=MESH,
            ).start()

    def wait_rows(slot, count):
        pltpu.make_async_copy(
            rows.at[slot, pl.ds(0, blocks - 1)], rows.at[slot, pl.ds(0, blocks - 1)], row_recv_sem.at[slot]
        ).wait()
        total = jnp.sum(rows[slot], axis=0)
        return [total[:, n:n + 1] / cells for n in range(count)]

    def wait_rows_sent(slot):
        pltpu.make_async_copy(
            rows.at[slot, pl.ds(0, blocks - 1)], rows.at[slot, pl.ds(0, blocks - 1)], row_send_sem.at[slot]
        ).wait()

    def inner(a, b):
        return jnp.sum(jnp.sum(a * b, axis=0, keepdims=True), axis=1, keepdims=True)

    places = []
    for j in range(1, nsrc):
        offset = ids_ref[j] - me
        places.append(jnp.where(offset == -1, 0, jnp.where(offset == 1, 1, jnp.where(offset == -GRID, 2, 3))))
    alive = [(j < live_ref[0]).astype(F32) for j in range(nsrc)]

    def multiply(pieces, wait):
        total = jnp.zeros((width, width), F32)
        blank = jnp.zeros((width, width), BF16)
        for i, (p, g) in enumerate(steps):
            if wait:
                pltpu.make_async_copy(span(renv, p, g), span(renv, p, g), renv_sem.at[i]).wait()
                pltpu.make_async_copy(span(env, p, g), span(env, p, g), env_recv.at[i]).wait()
            weights = jnp.concatenate([
                jnp.concatenate([pieces[2 * p], blank], axis=1),
                jnp.concatenate([blank, pieces[2 * p + 1]], axis=1),
            ], axis=0)
            at = slice(g * GROUP * width, (g + 1) * GROUP * width)
            both = jnp.concatenate([env[2 * p, at, :], env[2 * p + 1, at, :]], axis=1)
            product = jnp.dot(both, weights, preferred_element_type=F32).astype(BF16)
            lhs = jnp.concatenate([product[w * width:(w + 1) * width] for w in range(GROUP)], axis=1)
            rhs = []
            for w in range(GROUP):
                at = slice((g * GROUP + w) * width, (g * GROUP + w + 1) * width)
                rhs += [renv[2 * p, at, :], renv[2 * p + 1, at, :]]
            total = total + jnp.dot(lhs, jnp.concatenate(rhs, axis=0), preferred_element_type=F32)
        return total

    for n in range(4):
        start_copy(n).start()
    start = start_ref[...]
    send_rows([inner(start, start)], 1)
    for n in range(4):
        start_copy(n).wait()
    (norm,) = wait_rows(1, 1)
    wait_rows_sent(1)
    scale = lax.rsqrt(norm + EPS)
    xx_start = norm / (norm + EPS)
    pieces = []
    for j in range(nsrc):
        block = (start if j == 0 else start_halo[places[j - 1]]) * scale
        ts[j] = block
        xs[j] = jnp.zeros((width, width), F32)
        ys[j] = jnp.zeros((width, width), F32)
        pieces.append((block * alive[j]).astype(BF16))

    def share(z, slot, halo):
        zown[...] = z
        if halo:
            zsend[slot] = z.astype(HALO)
            for n in range(4):
                halo_copy(n, slot).start()
        send_rows([inner(xs[0], z), inner(ts[0], z), inner(ys[0], z), inner(z, z)], slot)

    def rotate(slot, first, a, xx, yy, tt, inv):
        xz, tz, yz, zz = wait_rows(slot, 4)
        off = 0.5 * ((yy - a * a) * inv + xz)
        gap = 0.5 * (a - tz)
        size = jnp.sqrt(gap * gap + off * off)
        energy = 0.5 * (a + tz) - size
        safe = jnp.where(size > 0, size, 1.0)
        major = jnp.sqrt(0.5 + 0.5 * jnp.abs(gap) / safe)
        minor = jnp.abs(off) / safe / (2.0 * major)
        cosine = jnp.where(gap <= 0, major, minor)
        sine = jnp.where(gap <= 0, minor, major) * jnp.where(off >= 0, -1.0, 1.0)
        cosine = jnp.where(first, 0.0, cosine)
        sine = jnp.where(first, 1.0, sine)
        cc, cs, ss = cosine * cosine, cosine * sine, sine * sine
        xt = a * (1.0 - xx) * inv
        new_a = cc * a + 2.0 * cs * off + ss * tz
        new_yy = cc * yy + 2.0 * cs * yz + ss * zz
        new_xx = cc * xx + 2.0 * cs * xt + ss * tt
        rho = jnp.maximum(new_yy - 2.0 * new_a * new_a + new_a * new_a * new_xx, 0.0)
        new_inv = lax.rsqrt(rho + EPS)
        return energy, cosine, sine, new_a, new_xx, new_yy, rho / (rho + EPS), new_inv

    share(multiply(pieces, True), 0, True)

    def round_of(slot, first, carry):
        a, xx, yy, tt, inv = carry
        _, cosine, sine, a, xx, yy, tt, inv = rotate(slot, first, a, xx, yy, tt, inv)
        for n in range(4):
            halo_copy(n, slot).wait()
        wait_rows_sent(slot)
        pieces = []
        for j in range(nsrc):
            z = zown[...] if j == 0 else zhalo[slot][places[j - 1]].astype(F32)
            x = cosine * xs[j] + sine * ts[j]
            y = cosine * ys[j] + sine * z
            t = (y - a * x) * inv
            xs[j] = x
            ys[j] = y
            ts[j] = t
            pieces.append((t * alive[j]).astype(BF16))
        z = multiply(pieces, False)
        share(z, 1 - slot, True)
        return a, xx, yy, tt, inv

    zero = jnp.zeros((1, 1), F32)
    carry = lax.fori_loop(
        0, ITERS // 2,
        lambda k, carry: round_of(1, False, round_of(0, k == 0, carry)),
        (zero, zero, zero, xx_start, zero + 1.0),
    )
    slot = ITERS % 2
    energy, cosine, sine, *_ = rotate(slot, False, *carry)
    state_ref[...] = cosine * xs[0] + sine * ts[0]
    energy_ref[0] = energy[0, 0]
    for n in range(4):
        halo_copy(n, slot).wait()
    wait_rows_sent(slot)

    @pl.when(site < sites - 1)
    def _():
        for i, (p, g) in enumerate(steps):
            env_copy(i, p, g).wait_send()


def per_device(initial_state, left_env, edge_env, right_env, source_blocks, live_terms):
    nsrc, terms, width = left_env.shape[2], left_env.shape[3], left_env.shape[4]
    blocks, sites = lax.axis_size("sector"), lax.axis_size("site")
    count = (nsrc // 2) * (terms // GROUP)
    flat = (nsrc, terms * width, width)
    vmem = pl.BlockSpec(memory_space=pltpu.VMEM)
    smem = pl.BlockSpec(memory_space=pltpu.SMEM)
    anywhere = pl.BlockSpec(memory_space=pl.ANY)
    dma = pltpu.SemaphoreType.DMA
    body = functools.partial(kernel, blocks, float(blocks * width * width), sites, nsrc, terms)
    state, energy = pl.pallas_call(
        body,
        out_shape=(
            jax.ShapeDtypeStruct((width, width), F32),
            jax.ShapeDtypeStruct((1,), F32),
        ),
        in_specs=[vmem, anywhere, anywhere, anywhere, smem, smem],
        out_specs=(vmem, smem),
        scratch_shapes=[
            pltpu.VMEM(flat, BF16),
            pltpu.VMEM(flat, BF16),
            pltpu.VMEM((nsrc, width, width), F32),
            pltpu.VMEM((nsrc, width, width), F32),
            pltpu.VMEM((nsrc, width, width), F32),
            pltpu.VMEM((width, width), F32),
            pltpu.VMEM((4, width, width), F32),
            pltpu.VMEM((2, width, width), HALO),
            pltpu.VMEM((4, width, width), HALO),
            pltpu.VMEM((4, width, width), HALO),
            pltpu.VMEM((2, 1, width), F32),
            pltpu.VMEM((2, blocks, 1, width), F32),
            dma((count,)), dma((count,)), dma((count,)), dma((4,)), dma((4,)),
            dma((2, 4)), dma((2, 4)), dma((2,)), dma((2,)),
        ],
        compiler_params=pltpu.CompilerParams(
            collective_id=0, has_side_effects=True, vmem_limit_bytes=32 * 1024 * 1024
        ),
        name="window",
    )(
        initial_state[0, 0],
        left_env.reshape(flat),
        edge_env.reshape(flat),
        right_env.reshape(flat),
        source_blocks.reshape(nsrc),
        live_terms.reshape(1),
    )
    return state[None, None], energy


def solution(mesh):
    placed = (
        P("site", "sector", None, None),
        P("site", "sector", None, None, None, None),
        P("sector", None, None, None, None),
        P("site", "sector", None, None, None, None),
        P("site", "sector", None),
        P("site", "sector"),
    )
    return jax.shard_map(
        per_device,
        mesh=mesh,
        in_specs=placed,
        out_specs=(P("site", "sector", None, None), P("site")),
        check_vma=False,
    )
```

```python
import functools

import jax
import jax.numpy as jnp
from jax import lax
from jax.experimental import pallas as pl
from jax.experimental.pallas import tpu as pltpu
from jax.sharding import PartitionSpec as P

GRID = 4
ITERS = 8
GROUP = 3
LATE_FIRST = 3
HALO = jnp.bfloat16
PART = jnp.bfloat16
EPS = 1e-06
MESH = pl.DeviceIdType.MESH
F32 = jnp.float32
BF16 = jnp.bfloat16


def kernel(
    blocks, cells, sites, nsrc, terms,
    start_ref, left_ref, edge_ref, right_ref, ids_ref, live_ref,
    state_ref, energy_ref,
    env, renv, help_env, help_renv, xs, ys, ts, zown, start_halo, zsend, zhalo_even, zhalo_odd, row_send, rows,
    piece_send, piece_in, part_send, part_in,
    env_send, env_recv, renv_sem, start_sem, start_send, start_recv,
    halo_send, halo_recv, row_send_sem, row_recv_sem,
    help_env_sem, help_renv_send, help_renv_recv, piece_sends, piece_recvs, part_sends, part_recvs,
):
    site = lax.axis_index("site")
    me = lax.axis_index("sector")
    width = start_ref.shape[-1]
    groups = terms // GROUP
    steps = [(p, g) for p in range(nsrc // 2) for g in range(groups)]
    early = [i for i, (p, _) in enumerate(steps) if p == 0]
    late = [i for i, (p, _) in enumerate(steps) if p == 1]
    first_site, last_site = site == 0, site == sites - 1

    def peer(by):
        return lax.rem(me + by + blocks, blocks)

    barrier = pltpu.get_barrier_semaphore()

    @pl.when(site > 0)
    def _():
        pl.semaphore_signal(barrier, inc=1, device_id={"site": site - 1}, device_id_type=MESH)

    @pl.when(site < sites - 1)
    def _():
        pl.semaphore_signal(barrier, inc=1, device_id={"site": site + 1}, device_id_type=MESH)

    for d in range(1, blocks):
        pl.semaphore_signal(barrier, inc=1, device_id={"sector": peer(d)}, device_id_type=MESH)

    def span(ref, p, g):
        return ref.at[pl.ds(2 * p, 2), pl.ds(g * GROUP * width, GROUP * width), :]

    pltpu.make_async_copy(start_ref, zown, start_sem).start()
    for i, (p, g) in enumerate(steps):
        pltpu.make_async_copy(span(right_ref, p, g), span(renv, p, g), renv_sem.at[i]).start()

    @pl.when(first_site)
    def _():
        for i, (p, g) in enumerate(steps):
            pltpu.make_async_copy(span(edge_ref, p, g), span(env, p, g), env_recv.at[i]).start()

    @pl.when(jnp.logical_not(last_site))
    def _():
        pltpu.make_async_copy(left_ref.at[pl.ds(2, 2)], help_env, help_env_sem).start()

    pl.semaphore_wait(
        barrier, blocks - 1 + jnp.where(site > 0, 1, 0) + jnp.where(site < sites - 1, 1, 0)
    )

    def env_copy(i):
        p, g = steps[i]
        return pltpu.make_async_remote_copy(
            src_ref=span(left_ref, p, g), dst_ref=span(env, p, g),
            send_sem=env_send.at[i], recv_sem=env_recv.at[i],
            device_id={"site": site + 1}, device_id_type=MESH,
        )

    def help_copy(g):
        return pltpu.make_async_remote_copy(
            src_ref=span(right_ref, 1, g), dst_ref=span(help_renv, 0, g),
            send_sem=help_renv_send.at[g], recv_sem=help_renv_recv.at[g],
            device_id={"site": site - 1}, device_id_type=MESH,
        )

    def piece_copy(n):
        return pltpu.make_async_remote_copy(
            src_ref=piece_send.at[n], dst_ref=piece_in.at[n],
            send_sem=piece_sends.at[n], recv_sem=piece_recvs.at[n],
            device_id={"site": site - 1}, device_id_type=MESH,
        )

    def part_copy(n):
        return pltpu.make_async_remote_copy(
            src_ref=part_send.at[n], dst_ref=part_in.at[n],
            send_sem=part_sends.at[n], recv_sem=part_recvs.at[n],
            device_id={"site": site + 1}, device_id_type=MESH,
        )

    @pl.when(jnp.logical_not(last_site))
    def _():
        for i in early:
            env_copy(i).start()

    @pl.when(jnp.logical_not(first_site))
    def _():
        for g in range(groups - 1):
            help_copy(g).start()

    hops = (1, -1, GRID, -GRID)
    zhalo = (zhalo_even, zhalo_odd)

    def start_copy(n):
        return pltpu.make_async_remote_copy(
            src_ref=start_ref, dst_ref=start_halo.at[n],
            send_sem=start_send.at[n], recv_sem=start_recv.at[n],
            device_id={"sector": peer(hops[n])}, device_id_type=MESH,
        )

    def halo_copy(n, slot):
        return pltpu.make_async_remote_copy(
            src_ref=zsend.at[slot], dst_ref=zhalo[slot].at[n],
            send_sem=halo_send.at[slot, n], recv_sem=halo_recv.at[slot, n],
            device_id={"sector": peer(hops[n])}, device_id_type=MESH,
        )

    def send_rows(values, slot):
        lane = lax.broadcasted_iota(jnp.int32, (1, width), 1)
        row = jnp.zeros((1, width), F32)
        for n, value in enumerate(values):
            row = jnp.where(lane == n, value, row)
        row_send[slot] = row
        rows[slot, me] = row
        for d in range(1, blocks):
            pltpu.make_async_remote_copy(
                src_ref=row_send.at[slot], dst_ref=rows.at[slot, me],
                send_sem=row_send_sem.at[slot], recv_sem=row_recv_sem.at[slot],
                device_id={"sector": peer(d)}, device_id_type=MESH,
            ).start()

    def wait_rows(slot, count):
        pltpu.make_async_copy(
            rows.at[slot, pl.ds(0, blocks - 1)], rows.at[slot, pl.ds(0, blocks - 1)], row_recv_sem.at[slot]
        ).wait()
        total = jnp.sum(rows[slot], axis=0)
        return [total[:, n:n + 1] / cells for n in range(count)]

    def wait_rows_sent(slot):
        pltpu.make_async_copy(
            rows.at[slot, pl.ds(0, blocks - 1)], rows.at[slot, pl.ds(0, blocks - 1)], row_send_sem.at[slot]
        ).wait()

    def inner(a, b):
        return jnp.sum(jnp.sum(a * b, axis=0, keepdims=True), axis=1, keepdims=True)

    places = []
    for j in range(1, nsrc):
        offset = ids_ref[j] - me
        places.append(jnp.where(offset == -1, 0, jnp.where(offset == 1, 1, jnp.where(offset == -GRID, 2, 3))))
    alive = [(j < live_ref[0]).astype(F32) for j in range(nsrc)]

    def multiply(total, e_ref, r_ref, p, two, wait=None):
        size = GROUP if wait else terms
        blank = jnp.zeros((width, width), BF16)
        weights = jnp.concatenate([
            jnp.concatenate([two[0], blank], axis=1),
            jnp.concatenate([blank, two[1]], axis=1),
        ], axis=0)
        for g in range(terms // size):
            if wait:
                wait(g)
            at = slice(g * size * width, (g + 1) * size * width)
            both = jnp.concatenate([e_ref[2 * p, at, :], e_ref[2 * p + 1, at, :]], axis=1)
            product = jnp.dot(both, weights, preferred_element_type=F32).astype(BF16)
            lhs = jnp.concatenate([product[w * width:(w + 1) * width] for w in range(size)], axis=1)
            rhs = []
            for w in range(size):
                at = slice((g * size + w) * width, (g * size + w + 1) * width)
                rhs += [r_ref[2 * p, at, :], r_ref[2 * p + 1, at, :]]
            total = total + jnp.dot(lhs, jnp.concatenate(rhs, axis=0), preferred_element_type=F32)
        return total

    def wait_env(i):
        pltpu.make_async_copy(span(env, *steps[i]), span(env, *steps[i]), env_recv.at[i]).wait()

    nothing = jnp.zeros((width, width), F32)

    def shared_multiply(n, pieces):
        piece_send[n, 0] = pieces[2]
        piece_send[n, 1] = pieces[3]

        @pl.when(jnp.logical_not(first_site))
        def _():
            piece_copy(n).start()
            if n == 0:
                help_copy(groups - 1).start()

        @pl.when(jnp.logical_not(last_site))
        def _():
            piece = pltpu.make_async_copy(piece_in.at[n], piece_in.at[n], piece_recvs.at[n])
            piece.wait()
            if n == 0:
                pltpu.make_async_copy(help_env, help_env, help_env_sem).wait()

            def arrived(g):
                pltpu.make_async_copy(
                    span(help_renv, 0, g), span(help_renv, 0, g), help_renv_recv.at[g]
                ).wait()

            part_send[n] = multiply(
                nothing, help_env, help_renv, 0, [piece_in[n, 0], piece_in[n, 1]], None if n else arrived
            ).astype(PART)
            part_copy(n).start()
            for i in (late[:LATE_FIRST], late[LATE_FIRST:])[n]:
                env_copy(i).start()

        if n == 0:
            for i, (p, g) in enumerate(steps):
                pltpu.make_async_copy(span(renv, p, g), span(renv, p, g), renv_sem.at[i]).wait()
        total = multiply(
            nothing, env, renv, 0, pieces[:2], None if n else lambda g: wait_env(early[g])
        )

        @pl.when(first_site)
        def _():
            if n == 0:
                for i in late:
                    wait_env(i)
            part_in[n] = multiply(nothing, env, renv, 1, pieces[2:]).astype(PART)

        @pl.when(jnp.logical_not(first_site))
        def _():
            pltpu.make_async_copy(part_in.at[n], part_in.at[n], part_recvs.at[n]).wait()

        return total + part_in[n].astype(F32)

    def local_multiply(pieces, wait):
        total = multiply(nothing, env, renv, 0, pieces[:2])
        if wait:
            @pl.when(jnp.logical_not(first_site))
            def _():
                for i in late:
                    wait_env(i)
        return multiply(total, env, renv, 1, pieces[2:])

    for n in range(4):
        start_copy(n).start()
    pltpu.make_async_copy(start_ref, zown, start_sem).wait()
    start = zown[...]
    send_rows([inner(start, start)], 1)
    for n in range(4):
        start_copy(n).wait()
    (norm,) = wait_rows(1, 1)
    wait_rows_sent(1)
    scale = lax.rsqrt(norm + EPS)
    xx_start = norm / (norm + EPS)
    pieces = []
    for j in range(nsrc):
        block = (start if j == 0 else start_halo[places[j - 1]]) * scale
        ts[j] = block
        xs[j] = jnp.zeros((width, width), F32)
        ys[j] = jnp.zeros((width, width), F32)
        pieces.append((block * alive[j]).astype(BF16))

    def share(z, slot, halo):
        zown[...] = z
        if halo:
            zsend[slot] = z.astype(HALO)
            for n in range(4):
                halo_copy(n, slot).start()
        send_rows([inner(xs[0], z), inner(ts[0], z), inner(ys[0], z), inner(z, z)], slot)

    def rotate(slot, first, a, xx, yy, tt, inv):
        xz, tz, yz, zz = wait_rows(slot, 4)
        off = 0.5 * ((yy - a * a) * inv + xz)
        gap = 0.5 * (a - tz)
        square = gap * gap + off * off
        over = jnp.where(square > 0, lax.rsqrt(jnp.where(square > 0, square, 1.0)), 0.0)
        energy = 0.5 * (a + tz) - square * over
        half = 0.5 + 0.5 * jnp.abs(gap) * over
        turn = lax.rsqrt(half)
        major = half * turn
        minor = 0.5 * jnp.abs(off) * over * turn
        cosine = jnp.where(gap <= 0, major, minor)
        sine = jnp.where(gap <= 0, minor, major) * jnp.where(off >= 0, -1.0, 1.0)
        if first:
            cosine, sine = jnp.zeros_like(gap), jnp.ones_like(gap)
        cc, cs, ss = cosine * cosine, cosine * sine, sine * sine
        xt = a * (1.0 - xx) * inv
        new_a = cc * a + 2.0 * cs * off + ss * tz
        new_yy = cc * yy + 2.0 * cs * yz + ss * zz
        new_xx = cc * xx + 2.0 * cs * xt + ss * tt
        rho = jnp.maximum(new_yy - 2.0 * new_a * new_a + new_a * new_a * new_xx, 0.0)
        new_inv = lax.rsqrt(rho + EPS)
        return energy, cosine, sine, new_a, new_xx, new_yy, rho / (rho + EPS), new_inv

    share(shared_multiply(0, pieces), 0, True)

    def round_of(slot, first, carry, apply):
        a, xx, yy, tt, inv = carry
        _, cosine, sine, a, xx, yy, tt, inv = rotate(slot, first, a, xx, yy, tt, inv)
        for n in range(4):
            halo_copy(n, slot).wait_recv()
        pieces = []
        for j in range(nsrc):
            z = zown[...] if j == 0 else zhalo[slot][places[j - 1]].astype(F32)
            x = cosine * xs[j] + sine * ts[j]
            y = cosine * ys[j] + sine * z
            t = (y - a * x) * inv
            xs[j] = x
            ys[j] = y
            ts[j] = t
            pieces.append((t * alive[j]).astype(BF16))
        z = apply(pieces)
        for n in range(4):
            halo_copy(n, slot).wait_send()
        wait_rows_sent(slot)
        share(z, 1 - slot, True)
        return a, xx, yy, tt, inv

    zero = jnp.zeros((1, 1), F32)
    carry = (zero, zero, zero, xx_start, zero + 1.0)
    carry = round_of(0, True, carry, lambda pieces: shared_multiply(1, pieces))
    carry = round_of(1, False, carry, lambda pieces: local_multiply(pieces, True))

    def two_rounds(_, carry):
        for slot in range(2):
            carry = round_of(slot, False, carry, lambda pieces: local_multiply(pieces, False))
        return carry

    carry = lax.fori_loop(0, ITERS // 2 - 1, two_rounds, carry)
    slot = ITERS % 2
    energy, cosine, sine, *_ = rotate(slot, False, *carry)
    state_ref[...] = cosine * xs[0] + sine * ts[0]
    energy_ref[0] = energy[0, 0]
    for n in range(4):
        halo_copy(n, slot).wait()
    wait_rows_sent(slot)

    @pl.when(jnp.logical_not(last_site))
    def _():
        for i in range(len(steps)):
            env_copy(i).wait_send()
        for n in range(2):
            part_copy(n).wait_send()

    @pl.when(jnp.logical_not(first_site))
    def _():
        for g in range(groups):
            help_copy(g).wait_send()
        for n in range(2):
            piece_copy(n).wait_send()


def per_device(initial_state, left_env, edge_env, right_env, source_blocks, live_terms):
    nsrc, terms, width = left_env.shape[2], left_env.shape[3], left_env.shape[4]
    blocks, sites = lax.axis_size("sector"), lax.axis_size("site")
    count = (nsrc // 2) * (terms // GROUP)
    flat = (nsrc, terms * width, width)
    vmem = pl.BlockSpec(memory_space=pltpu.VMEM)
    smem = pl.BlockSpec(memory_space=pltpu.SMEM)
    anywhere = pl.BlockSpec(memory_space=pl.ANY)
    dma = pltpu.SemaphoreType.DMA
    body = functools.partial(kernel, blocks, float(blocks * width * width), sites, nsrc, terms)
    state, energy = pl.pallas_call(
        body,
        out_shape=(
            jax.ShapeDtypeStruct((width, width), F32),
            jax.ShapeDtypeStruct((1,), F32),
        ),
        in_specs=[anywhere, anywhere, anywhere, anywhere, smem, smem],
        out_specs=(vmem, smem),
        scratch_shapes=[
            pltpu.VMEM(flat, BF16),
            pltpu.VMEM(flat, BF16),
            pltpu.VMEM((2, *flat[1:]), BF16),
            pltpu.VMEM((2, *flat[1:]), BF16),
            pltpu.VMEM((nsrc, width, width), F32),
            pltpu.VMEM((nsrc, width, width), F32),
            pltpu.VMEM((nsrc, width, width), F32),
            pltpu.VMEM((width, width), F32),
            pltpu.VMEM((4, width, width), F32),
            pltpu.VMEM((2, width, width), HALO),
            pltpu.VMEM((4, width, width), HALO),
            pltpu.VMEM((4, width, width), HALO),
            pltpu.VMEM((2, 1, width), F32),
            pltpu.VMEM((2, blocks, 1, width), F32),
            pltpu.VMEM((2, 2, width, width), BF16),
            pltpu.VMEM((2, 2, width, width), BF16),
            pltpu.VMEM((2, width, width), PART),
            pltpu.VMEM((2, width, width), PART),
            dma((count,)), dma((count,)), dma((count,)), dma, dma((4,)), dma((4,)),
            dma((2, 4)), dma((2, 4)), dma((2,)), dma((2,)),
            dma, dma((count // 2,)), dma((count // 2,)), dma((2,)), dma((2,)), dma((2,)), dma((2,)),
        ],
        compiler_params=pltpu.CompilerParams(
            collective_id=0, has_side_effects=True, vmem_limit_bytes=60 * 1024 * 1024
        ),
        name="window",
    )(
        initial_state[0, 0],
        left_env.reshape(flat),
        edge_env.reshape(flat),
        right_env.reshape(flat),
        source_blocks.reshape(nsrc),
        live_terms.reshape(1),
    )
    return state[None, None], energy


def solution(mesh):
    placed = (
        P("site", "sector", None, None),
        P("site", "sector", None, None, None, None),
        P("sector", None, None, None, None),
        P("site", "sector", None, None, None, None),
        P("site", "sector", None),
        P("site", "sector"),
    )
    return jax.shard_map(
        per_device,
        mesh=mesh,
        in_specs=placed,
        out_specs=(P("site", "sector", None, None), P("site")),
        check_vma=False,
    )
```

```python
import functools

import jax
import jax.numpy as jnp
from jax import lax
from jax.experimental import pallas as pl
from jax.experimental.pallas import tpu as pltpu
from jax.sharding import PartitionSpec as P

GRID = 4
ITERS = 8
GROUP = 3
LATE_FIRST = 3
HALO = jnp.bfloat16
PART = jnp.bfloat16
EPS = 1e-06
MESH = pl.DeviceIdType.MESH
F32 = jnp.float32
BF16 = jnp.bfloat16


def kernel(
    blocks, cells, sites, nsrc, terms,
    start_ref, left_ref, edge_ref, right_ref, ids_ref, live_ref,
    state_ref, energy_ref,
    env, renv, help_env, help_renv, xs, ys, us, ts, zs, start_halo, zsend, zhalo_even, zhalo_odd, row_send, rows, norm_send, norms,
    piece_send, piece_in, part_send, part_in,
    env_send, env_recv, renv_sem, start_sem, start_send, start_recv,
    halo_send, halo_recv, row_send_sem, row_recv_sem, norm_send_sem, norm_recv_sem,
    help_env_sem, help_renv_send, help_renv_recv, piece_sends, piece_recvs, part_sends, part_recvs,
):
    site = lax.axis_index("site")
    me = lax.axis_index("sector")
    width = start_ref.shape[-1]
    groups = terms // GROUP
    steps = [(p, g) for p in range(nsrc // 2) for g in range(groups)]
    early = [i for i, (p, _) in enumerate(steps) if p == 0]
    late = [i for i, (p, _) in enumerate(steps) if p == 1]
    first_site, last_site = site == 0, site == sites - 1

    def peer(by):
        return lax.rem(me + by + blocks, blocks)

    barrier = pltpu.get_barrier_semaphore()

    @pl.when(site > 0)
    def _():
        pl.semaphore_signal(barrier, inc=1, device_id={"site": site - 1}, device_id_type=MESH)

    @pl.when(site < sites - 1)
    def _():
        pl.semaphore_signal(barrier, inc=1, device_id={"site": site + 1}, device_id_type=MESH)

    side = 2 * GRID
    base, spot, line = me - lax.rem(me, side), lax.rem(me, side), me // side
    planes = ([base + lax.rem(spot + d, side) for d in range(1, side)], [peer(d) for d in range(side, blocks, side)])
    for other in planes[0] + planes[1]:
        pl.semaphore_signal(barrier, inc=1, device_id={"sector": other}, device_id_type=MESH)

    def span(ref, p, g):
        return ref.at[pl.ds(2 * p, 2), pl.ds(g * GROUP * width, GROUP * width), :]

    pltpu.make_async_copy(start_ref, zs, start_sem).start()
    for i, (p, g) in enumerate(steps):
        pltpu.make_async_copy(span(right_ref, p, g), span(renv, p, g), renv_sem.at[i]).start()

    @pl.when(first_site)
    def _():
        for i, (p, g) in enumerate(steps):
            pltpu.make_async_copy(span(edge_ref, p, g), span(env, p, g), env_recv.at[i]).start()

    @pl.when(jnp.logical_not(last_site))
    def _():
        pltpu.make_async_copy(left_ref.at[pl.ds(2, 2)], help_env, help_env_sem).start()

    pl.semaphore_wait(
        barrier, len(planes[0]) + len(planes[1]) + jnp.where(site > 0, 1, 0) + jnp.where(site < sites - 1, 1, 0)
    )

    def env_copy(i):
        p, g = steps[i]
        return pltpu.make_async_remote_copy(
            src_ref=span(left_ref, p, g), dst_ref=span(env, p, g),
            send_sem=env_send.at[i], recv_sem=env_recv.at[i],
            device_id={"site": site + 1}, device_id_type=MESH,
        )

    def help_copy(g):
        return pltpu.make_async_remote_copy(
            src_ref=span(right_ref, 1, g), dst_ref=span(help_renv, 0, g),
            send_sem=help_renv_send.at[g], recv_sem=help_renv_recv.at[g],
            device_id={"site": site - 1}, device_id_type=MESH,
        )

    def piece_copy(n):
        return pltpu.make_async_remote_copy(
            src_ref=piece_send.at[n], dst_ref=piece_in.at[n],
            send_sem=piece_sends.at[n], recv_sem=piece_recvs.at[n],
            device_id={"site": site - 1}, device_id_type=MESH,
        )

    def part_copy(n):
        return pltpu.make_async_remote_copy(
            src_ref=part_send.at[n], dst_ref=part_in.at[n],
            send_sem=part_sends.at[n], recv_sem=part_recvs.at[n],
            device_id={"site": site + 1}, device_id_type=MESH,
        )

    @pl.when(jnp.logical_not(last_site))
    def _():
        for i in early:
            env_copy(i).start()

    @pl.when(jnp.logical_not(first_site))
    def _():
        for g in range(groups - 1):
            help_copy(g).start()

    hops = (1, -1, GRID, -GRID)
    zhalo = (zhalo_even, zhalo_odd)

    def start_copy(n):
        return pltpu.make_async_remote_copy(
            src_ref=start_ref, dst_ref=start_halo.at[n],
            send_sem=start_send.at[n], recv_sem=start_recv.at[n],
            device_id={"sector": peer(hops[n])}, device_id_type=MESH,
        )

    def halo_copy(n, slot):
        return pltpu.make_async_remote_copy(
            src_ref=zsend.at[slot], dst_ref=zhalo[slot].at[n],
            send_sem=halo_send.at[slot, n], recv_sem=halo_recv.at[slot, n],
            device_id={"sector": peer(hops[n])}, device_id_type=MESH,
        )

    far_first = sorted(range(1, blocks), key=lambda d: abs(d - blocks // 2))

    def send_rows(values, slot):
        lane = lax.broadcasted_iota(jnp.int32, (1, width), 1)
        row = jnp.zeros((1, width), F32)
        for n, value in enumerate(values):
            row = jnp.where(lane == n, value, row)
        row_send[slot] = row
        rows[slot, me] = row
        for d in far_first:
            pltpu.make_async_remote_copy(
                src_ref=row_send.at[slot], dst_ref=rows.at[slot, me],
                send_sem=row_send_sem.at[slot], recv_sem=row_recv_sem.at[slot],
                device_id={"sector": peer(d)}, device_id_type=MESH,
            ).start()

    def wait_rows(slot, count):
        pltpu.make_async_copy(
            rows.at[slot, pl.ds(0, blocks - 1)], rows.at[slot, pl.ds(0, blocks - 1)], row_recv_sem.at[slot]
        ).wait()
        total = jnp.sum(rows[slot], axis=0)
        return [total[:, n:n + 1] / cells for n in range(count)]

    def wait_rows_sent(slot):
        pltpu.make_async_copy(
            rows.at[slot, pl.ds(0, blocks - 1)], rows.at[slot, pl.ds(0, blocks - 1)], row_send_sem.at[slot]
        ).wait()

    def inner(a, b):
        return jnp.sum(jnp.sum(a * b, axis=0, keepdims=True), axis=1, keepdims=True)

    places = []
    for j in range(1, nsrc):
        offset = ids_ref[j] - me
        places.append(jnp.where(offset == -1, 0, jnp.where(offset == 1, 1, jnp.where(offset == -GRID, 2, 3))))
    alive = [(j < live_ref[0]).astype(F32) for j in range(nsrc)]

    def multiply(total, e_ref, r_ref, jobs, wait=None):
        size = GROUP if wait else terms
        for g in range(terms // size):
            if wait:
                wait(g)
            at = slice(g * size * width, (g + 1) * size * width)
            products = [
                jnp.dot(e_ref[j, at, :], piece, preferred_element_type=F32).astype(BF16) for j, piece in jobs
            ]
            for product, (j, _) in zip(products, jobs):
                lhs = jnp.concatenate([product[w * width:(w + 1) * width] for w in range(size)], axis=1)
                total = total + jnp.dot(lhs, r_ref[j, at, :], preferred_element_type=F32)
        return total

    def wait_env(i):
        pltpu.make_async_copy(span(env, *steps[i]), span(env, *steps[i]), env_recv.at[i]).wait()

    nothing = jnp.zeros((width, width), F32)

    def shared_multiply(n, total, pieces):
        piece_send[n, 0] = pieces[2]
        piece_send[n, 1] = pieces[3]

        @pl.when(jnp.logical_not(first_site))
        def _():
            piece_copy(n).start()
            if n == 0:
                help_copy(groups - 1).start()

        @pl.when(jnp.logical_not(last_site))
        def _():
            piece = pltpu.make_async_copy(piece_in.at[n], piece_in.at[n], piece_recvs.at[n])
            piece.wait()
            if n == 0:
                pltpu.make_async_copy(help_env, help_env, help_env_sem).wait()

            def arrived(g):
                pltpu.make_async_copy(
                    span(help_renv, 0, g), span(help_renv, 0, g), help_renv_recv.at[g]
                ).wait()

            part_send[n] = multiply(
                nothing, help_env, help_renv, [(0, piece_in[n, 0]), (1, piece_in[n, 1])], None if n else arrived
            ).astype(PART)
            part_copy(n).start()
            for i in (late[:LATE_FIRST], late[LATE_FIRST:])[n]:
                env_copy(i).start()

        if n == 0:
            for i, (p, g) in enumerate(steps):
                pltpu.make_async_copy(span(renv, p, g), span(renv, p, g), renv_sem.at[i]).wait()
        if n == 0:
            total = multiply(total, env, renv, [(0, pieces[0]), (1, pieces[1])], lambda g: wait_env(early[g]))
        else:
            total = multiply(total, env, renv, [(1, pieces[1])])

        @pl.when(first_site)
        def _():
            if n == 0:
                for i in late:
                    wait_env(i)
            part_in[n] = multiply(nothing, env, renv, [(2, pieces[2]), (3, pieces[3])]).astype(PART)

        @pl.when(jnp.logical_not(first_site))
        def _():
            pltpu.make_async_copy(part_in.at[n], part_in.at[n], part_recvs.at[n]).wait()

        return total + part_in[n].astype(F32)

    def local_multiply(total, pieces, wait):
        if wait:
            @pl.when(jnp.logical_not(first_site))
            def _():
                for i in late:
                    wait_env(i)
        return multiply(total, env, renv, [(j, pieces[j]) for j in range(1, nsrc)])

    pltpu.make_async_copy(start_ref, zs, start_sem).wait()
    start = zs[...]
    norm = inner(start, start)
    for stage, (others, own) in enumerate(zip(planes, (spot, line))):
        row = jnp.broadcast_to(norm, (1, width))
        count = len(others)
        norm_send[stage] = row
        norms[stage, own] = row
        for other in others:
            pltpu.make_async_remote_copy(
                src_ref=norm_send.at[stage], dst_ref=norms.at[stage, own],
                send_sem=norm_send_sem.at[stage], recv_sem=norm_recv_sem.at[stage],
                device_id={"sector": other}, device_id_type=MESH,
            ).start()
        came = norms.at[stage, pl.ds(0, count)]
        pltpu.make_async_copy(came, came, norm_recv_sem.at[stage]).wait()
        norm = jnp.sum(norms[stage, 0:count + 1], axis=0)[:, 0:1]
        pltpu.make_async_copy(came, came, norm_send_sem.at[stage]).wait()
    norm = norm / cells
    for n in range(4):
        start_copy(n).start()
    for n in range(4):
        start_copy(n).wait()
    scale = lax.rsqrt(norm + EPS)
    xx_start = norm / (norm + EPS)
    pieces = []
    for j in range(nsrc):
        block = (start if j == 0 else start_halo[places[j - 1]]) * scale
        if j == 0:
            ts[...] = block
        pieces.append((block * alive[j]).astype(BF16))
    for ref in (xs, ys, us):
        ref[...] = nothing

    def share(slot, halo):
        z = zs[...]
        zsend[slot] = z.astype(HALO)

        @pl.when(halo)
        def _():
            for n in range(4):
                halo_copy(n, slot).start()

        send_rows([inner(xs[...], z), inner(ts[...], z), inner(ys[...], z), inner(z, z)], slot)

    def rotate(slot, first, a, xx, yy, tt, inv):
        xz, tz, yz, zz = wait_rows(slot, 4)
        off = 0.5 * ((yy - a * a) * inv + xz)
        gap = 0.5 * (a - tz)
        square = gap * gap + off * off
        over = jnp.where(square > 0, lax.rsqrt(jnp.where(square > 0, square, 1.0)), 0.0)
        energy = 0.5 * (a + tz) - square * over
        half = 0.5 + 0.5 * jnp.abs(gap) * over
        turn = lax.rsqrt(half)
        major = half * turn
        minor = 0.5 * jnp.abs(off) * over * turn
        cosine = jnp.where(gap <= 0, major, minor)
        sine = jnp.where(gap <= 0, minor, major) * jnp.where(off >= 0, -1.0, 1.0)
        if first:
            cosine, sine = jnp.zeros_like(gap), jnp.ones_like(gap)
        cc, cs, ss = cosine * cosine, cosine * sine, sine * sine
        xt = a * (1.0 - xx) * inv
        new_a = cc * a + 2.0 * cs * off + ss * tz
        new_yy = cc * yy + 2.0 * cs * yz + ss * zz
        new_xx = cc * xx + 2.0 * cs * xt + ss * tt
        rho = jnp.maximum(new_yy - 2.0 * new_a * new_a + new_a * new_a * new_xx, 0.0)
        new_inv = lax.rsqrt(rho + EPS)
        return energy, cosine, sine, new_a, new_xx, new_yy, rho / (rho + EPS), new_inv

    zs[...] = shared_multiply(0, nothing, pieces)
    share(0, True)

    def round_of(slot, first, last, carry, apply):
        total = multiply(nothing, env, renv, [(0, zsend[slot])])
        for n in range(4):
            halo_copy(n, slot).wait_recv()
        pieces = [None]
        for j in range(1, nsrc):
            pieces.append((zhalo[slot][places[j - 1]].astype(F32) * alive[j]).astype(BF16))
        w = apply(total, pieces)
        a, xx, yy, tt, inv = carry
        _, cosine, sine, a, xx, yy, tt, inv = rotate(slot, first, a, xx, yy, tt, inv)
        x = cosine * xs[...] + sine * ts[...]
        y = cosine * ys[...] + sine * zs[...]
        u = cosine * us[...] + sine * w
        xs[...] = x
        ys[...] = y
        us[...] = u
        ts[...] = (y - a * x) * inv
        zs[...] = (u - a * y) * inv
        for n in range(4):
            halo_copy(n, slot).wait_send()
        wait_rows_sent(slot)
        share(1 - slot, jnp.logical_not(last))
        return a, xx, yy, tt, inv

    zero = jnp.zeros((1, 1), F32)
    carry = (zero, zero, zero, xx_start, zero + 1.0)
    carry = round_of(0, True, False, carry, lambda total, pieces: shared_multiply(1, total, pieces))
    carry = round_of(1, False, False, carry, lambda total, pieces: local_multiply(total, pieces, True))

    def two_rounds(k, carry):
        for slot in range(2):
            last = jnp.logical_and(slot == 1, k == ITERS // 2 - 2)
            carry = round_of(slot, False, last, carry, lambda total, pieces: local_multiply(total, pieces, False))
        return carry

    carry = lax.fori_loop(0, ITERS // 2 - 1, two_rounds, carry)
    slot = ITERS % 2
    energy, cosine, sine, *_ = rotate(slot, False, *carry)
    state_ref[...] = cosine * xs[...] + sine * ts[...]
    energy_ref[0] = energy[0, 0]
    wait_rows_sent(slot)

    @pl.when(jnp.logical_not(last_site))
    def _():
        for i in range(len(steps)):
            env_copy(i).wait_send()
        for n in range(2):
            part_copy(n).wait_send()

    @pl.when(jnp.logical_not(first_site))
    def _():
        for g in range(groups):
            help_copy(g).wait_send()
        for n in range(2):
            piece_copy(n).wait_send()


def per_device(initial_state, left_env, edge_env, right_env, source_blocks, live_terms):
    nsrc, terms, width = left_env.shape[2], left_env.shape[3], left_env.shape[4]
    blocks, sites = lax.axis_size("sector"), lax.axis_size("site")
    count = (nsrc // 2) * (terms // GROUP)
    flat = (nsrc, terms * width, width)
    vmem = pl.BlockSpec(memory_space=pltpu.VMEM)
    smem = pl.BlockSpec(memory_space=pltpu.SMEM)
    anywhere = pl.BlockSpec(memory_space=pl.ANY)
    dma = pltpu.SemaphoreType.DMA
    body = functools.partial(kernel, blocks, float(blocks * width * width), sites, nsrc, terms)
    state, energy = pl.pallas_call(
        body,
        out_shape=(
            jax.ShapeDtypeStruct((width, width), F32),
            jax.ShapeDtypeStruct((1,), F32),
        ),
        in_specs=[anywhere, anywhere, anywhere, anywhere, smem, smem],
        out_specs=(vmem, smem),
        scratch_shapes=[
            pltpu.VMEM(flat, BF16),
            pltpu.VMEM(flat, BF16),
            pltpu.VMEM((2, *flat[1:]), BF16),
            pltpu.VMEM((2, *flat[1:]), BF16),
            pltpu.VMEM((width, width), F32),
            pltpu.VMEM((width, width), F32),
            pltpu.VMEM((width, width), F32),
            pltpu.VMEM((width, width), F32),
            pltpu.VMEM((width, width), F32),
            pltpu.VMEM((4, width, width), F32),
            pltpu.VMEM((2, width, width), HALO),
            pltpu.VMEM((4, width, width), HALO),
            pltpu.VMEM((4, width, width), HALO),
            pltpu.VMEM((2, 1, width), F32),
            pltpu.VMEM((2, blocks, 1, width), F32),
            pltpu.VMEM((2, 1, width), F32),
            pltpu.VMEM((2, 2 * GRID, 1, width), F32),
            pltpu.VMEM((2, 2, width, width), BF16),
            pltpu.VMEM((2, 2, width, width), BF16),
            pltpu.VMEM((2, width, width), PART),
            pltpu.VMEM((2, width, width), PART),
            dma((count,)), dma((count,)), dma((count,)), dma, dma((4,)), dma((4,)),
            dma((2, 4)), dma((2, 4)), dma((2,)), dma((2,)), dma((2,)), dma((2,)),
            dma, dma((count // 2,)), dma((count // 2,)), dma((2,)), dma((2,)), dma((2,)), dma((2,)),
        ],
        compiler_params=pltpu.CompilerParams(
            collective_id=0, has_side_effects=True, vmem_limit_bytes=60 * 1024 * 1024
        ),
        name="window",
    )(
        initial_state[0, 0],
        left_env.reshape(flat),
        edge_env.reshape(flat),
        right_env.reshape(flat),
        source_blocks.reshape(nsrc),
        live_terms.reshape(1),
    )
    return state[None, None], energy


def solution(mesh):
    placed = (
        P("site", "sector", None, None),
        P("site", "sector", None, None, None, None),
        P("sector", None, None, None, None),
        P("site", "sector", None, None, None, None),
        P("site", "sector", None),
        P("site", "sector"),
    )
    return jax.shard_map(
        per_device,
        mesh=mesh,
        in_specs=placed,
        out_specs=(P("site", "sector", None, None), P("site")),
        check_vma=False,
    )
```

```python
import functools

import jax
import jax.numpy as jnp
from jax import lax
from jax.experimental import pallas as pl
from jax.experimental.pallas import tpu as pltpu
from jax.sharding import PartitionSpec as P

GRID = 4
ITERS = 8
GROUP = 2
LATE_FIRST = 4
HALO = jnp.bfloat16
PART = jnp.bfloat16
EPS = 1e-06
MESH = pl.DeviceIdType.MESH
F32 = jnp.float32
BF16 = jnp.bfloat16


def kernel(
    blocks, cells, sites, nsrc, terms,
    start_ref, left_ref, edge_ref, right_ref, ids_ref, live_ref,
    state_ref, energy_ref,
    env, renv, help_env, help_renv, xs, ys, us, ts, zs, start_halo, zsend, zhalo_even, zhalo_odd, row_send, rows, norm_send, norms,
    piece_send, piece_in, part_send, part_in,
    env_send, env_recv, renv_sem, start_sem, start_send, start_recv,
    halo_send, halo_recv, row_send_sem, row_recv_sem, norm_send_sem, norm_recv_sem,
    help_env_sem, help_renv_send, help_renv_recv, piece_sends, piece_recvs, part_sends, part_recvs,
):
    site = lax.axis_index("site")
    me = lax.axis_index("sector")
    width = start_ref.shape[-1]
    groups = terms // GROUP
    steps = [(p, g) for p in range(nsrc // 2) for g in range(groups)]
    early = [i for i, (p, _) in enumerate(steps) if p == 0]
    late = [i for i, (p, _) in enumerate(steps) if p == 1]
    first_site, last_site = site == 0, site == sites - 1

    def peer(by):
        return lax.rem(me + by + blocks, blocks)

    barrier = pltpu.get_barrier_semaphore()

    @pl.when(site > 0)
    def _():
        pl.semaphore_signal(barrier, inc=1, device_id={"site": site - 1}, device_id_type=MESH)

    @pl.when(site < sites - 1)
    def _():
        pl.semaphore_signal(barrier, inc=1, device_id={"site": site + 1}, device_id_type=MESH)

    side = 2 * GRID
    base, spot, line = me - lax.rem(me, side), lax.rem(me, side), me // side
    planes = ([base + lax.rem(spot + d, side) for d in range(1, side)], [peer(d) for d in range(side, blocks, side)])
    for other in planes[0] + planes[1]:
        pl.semaphore_signal(barrier, inc=1, device_id={"sector": other}, device_id_type=MESH)

    def span(ref, p, g):
        return ref.at[pl.ds(2 * p, 2), pl.ds(g * GROUP * width, GROUP * width), :]

    pltpu.make_async_copy(start_ref, zs, start_sem).start()
    for i, (p, g) in enumerate(steps):
        pltpu.make_async_copy(span(right_ref, p, g), span(renv, p, g), renv_sem.at[i]).start()

    @pl.when(first_site)
    def _():
        for i, (p, g) in enumerate(steps):
            pltpu.make_async_copy(span(edge_ref, p, g), span(env, p, g), env_recv.at[i]).start()

    @pl.when(jnp.logical_not(last_site))
    def _():
        pltpu.make_async_copy(left_ref.at[pl.ds(2, 2)], help_env, help_env_sem).start()

    pl.semaphore_wait(
        barrier, len(planes[0]) + len(planes[1]) + jnp.where(site > 0, 1, 0) + jnp.where(site < sites - 1, 1, 0)
    )

    def env_copy(i):
        p, g = steps[i]
        return pltpu.make_async_remote_copy(
            src_ref=span(left_ref, p, g), dst_ref=span(env, p, g),
            send_sem=env_send.at[i], recv_sem=env_recv.at[i],
            device_id={"site": site + 1}, device_id_type=MESH,
        )

    def help_copy(g):
        return pltpu.make_async_remote_copy(
            src_ref=span(right_ref, 1, g), dst_ref=span(help_renv, 0, g),
            send_sem=help_renv_send.at[g], recv_sem=help_renv_recv.at[g],
            device_id={"site": site - 1}, device_id_type=MESH,
        )

    def piece_copy(n):
        return pltpu.make_async_remote_copy(
            src_ref=piece_send.at[n], dst_ref=piece_in.at[n],
            send_sem=piece_sends.at[n], recv_sem=piece_recvs.at[n],
            device_id={"site": site - 1}, device_id_type=MESH,
        )

    def part_copy(n):
        return pltpu.make_async_remote_copy(
            src_ref=part_send.at[n], dst_ref=part_in.at[n],
            send_sem=part_sends.at[n], recv_sem=part_recvs.at[n],
            device_id={"site": site + 1}, device_id_type=MESH,
        )

    @pl.when(jnp.logical_not(last_site))
    def _():
        for i in early:
            env_copy(i).start()

    @pl.when(jnp.logical_not(first_site))
    def _():
        for g in range(groups - 1):
            help_copy(g).start()

    hops = (1, -1, GRID, -GRID)
    zhalo = (zhalo_even, zhalo_odd)

    def start_copy(n):
        return pltpu.make_async_remote_copy(
            src_ref=start_ref, dst_ref=start_halo.at[n],
            send_sem=start_send.at[n], recv_sem=start_recv.at[n],
            device_id={"sector": peer(hops[n])}, device_id_type=MESH,
        )

    def halo_copy(n, slot):
        return pltpu.make_async_remote_copy(
            src_ref=zsend.at[slot], dst_ref=zhalo[slot].at[n],
            send_sem=halo_send.at[slot, n], recv_sem=halo_recv.at[slot, n],
            device_id={"sector": peer(hops[n])}, device_id_type=MESH,
        )

    far_first = sorted(range(1, blocks), key=lambda d: abs(d - blocks // 2))

    def send_rows(values, slot):
        lane = lax.broadcasted_iota(jnp.int32, (1, width), 1)
        row = jnp.zeros((1, width), F32)
        for n, value in enumerate(values):
            row = jnp.where(lane == n, value, row)
        row_send[slot] = row
        rows[slot, me] = row
        for d in far_first:
            pltpu.make_async_remote_copy(
                src_ref=row_send.at[slot], dst_ref=rows.at[slot, me],
                send_sem=row_send_sem.at[slot], recv_sem=row_recv_sem.at[slot],
                device_id={"sector": peer(d)}, device_id_type=MESH,
            ).start()

    def wait_rows(slot, count):
        pltpu.make_async_copy(
            rows.at[slot, pl.ds(0, blocks - 1)], rows.at[slot, pl.ds(0, blocks - 1)], row_recv_sem.at[slot]
        ).wait()
        total = jnp.sum(rows[slot], axis=0)
        return [total[:, n:n + 1] / cells for n in range(count)]

    def wait_rows_sent(slot):
        pltpu.make_async_copy(
            rows.at[slot, pl.ds(0, blocks - 1)], rows.at[slot, pl.ds(0, blocks - 1)], row_send_sem.at[slot]
        ).wait()

    def inner(a, b):
        return jnp.sum(jnp.sum(a * b, axis=0, keepdims=True), axis=1, keepdims=True)

    places = []
    for j in range(1, nsrc):
        offset = ids_ref[j] - me
        places.append(jnp.where(offset == -1, 0, jnp.where(offset == 1, 1, jnp.where(offset == -GRID, 2, 3))))
    alive = [(j < live_ref[0]).astype(F32) for j in range(nsrc)]

    def multiply(total, e_ref, r_ref, jobs, wait=None):
        size = GROUP if wait else terms
        for g in range(terms // size):
            if wait:
                wait(g)
            at = slice(g * size * width, (g + 1) * size * width)
            products = [
                jnp.dot(e_ref[j, at, :], piece, preferred_element_type=F32).astype(BF16) for j, piece in jobs
            ]
            for product, (j, _) in zip(products, jobs):
                lhs = jnp.concatenate([product[w * width:(w + 1) * width] for w in range(size)], axis=1)
                total = total + jnp.dot(lhs, r_ref[j, at, :], preferred_element_type=F32)
        return total

    def wait_env(i):
        pltpu.make_async_copy(span(env, *steps[i]), span(env, *steps[i]), env_recv.at[i]).wait()

    nothing = jnp.zeros((width, width), F32)

    def shared_multiply(n, total, pieces):
        piece_send[n, 0] = pieces[2]
        piece_send[n, 1] = pieces[3]

        @pl.when(jnp.logical_not(first_site))
        def _():
            piece_copy(n).start()
            if n == 0:
                help_copy(groups - 1).start()

        @pl.when(jnp.logical_not(last_site))
        def _():
            piece = pltpu.make_async_copy(piece_in.at[n], piece_in.at[n], piece_recvs.at[n])
            piece.wait()
            if n == 0:
                pltpu.make_async_copy(help_env, help_env, help_env_sem).wait()

            def arrived(g):
                pltpu.make_async_copy(
                    span(help_renv, 0, g), span(help_renv, 0, g), help_renv_recv.at[g]
                ).wait()

            part_send[n] = multiply(
                nothing, help_env, help_renv, [(0, piece_in[n, 0]), (1, piece_in[n, 1])], None if n else arrived
            ).astype(PART)
            part_copy(n).start()
            for i in (late[:LATE_FIRST], late[LATE_FIRST:])[n]:
                env_copy(i).start()

        if n == 0:
            for i, (p, g) in enumerate(steps):
                pltpu.make_async_copy(span(renv, p, g), span(renv, p, g), renv_sem.at[i]).wait()
        if n == 0:
            total = multiply(total, env, renv, [(0, pieces[0]), (1, pieces[1])], lambda g: wait_env(early[g]))
        else:
            total = multiply(total, env, renv, [(1, pieces[1])])

        @pl.when(first_site)
        def _():
            if n == 0:
                for i in late:
                    wait_env(i)
            part_in[n] = multiply(nothing, env, renv, [(2, pieces[2]), (3, pieces[3])]).astype(PART)

        @pl.when(jnp.logical_not(first_site))
        def _():
            pltpu.make_async_copy(part_in.at[n], part_in.at[n], part_recvs.at[n]).wait()

        return total + part_in[n].astype(F32)

    def local_multiply(total, pieces, sums, wait):
        if wait:
            @pl.when(jnp.logical_not(first_site))
            def _():
                for i in late:
                    wait_env(i)
        total = multiply(total, env, renv, [(1, pieces[1])])
        turned = sums()
        return multiply(total, env, renv, [(j, pieces[j]) for j in range(2, nsrc)]), turned

    pltpu.make_async_copy(start_ref, zs, start_sem).wait()
    start = zs[...]
    norm = inner(start, start)
    for stage, (others, own) in enumerate(zip(planes, (spot, line))):
        row = jnp.broadcast_to(norm, (1, width))
        count = len(others)
        norm_send[stage] = row
        norms[stage, own] = row
        for other in others:
            pltpu.make_async_remote_copy(
                src_ref=norm_send.at[stage], dst_ref=norms.at[stage, own],
                send_sem=norm_send_sem.at[stage], recv_sem=norm_recv_sem.at[stage],
                device_id={"sector": other}, device_id_type=MESH,
            ).start()
        came = norms.at[stage, pl.ds(0, count)]
        pltpu.make_async_copy(came, came, norm_recv_sem.at[stage]).wait()
        norm = jnp.sum(norms[stage, 0:count + 1], axis=0)[:, 0:1]
        pltpu.make_async_copy(came, came, norm_send_sem.at[stage]).wait()
    norm = norm / cells
    for n in range(4):
        start_copy(n).start()
    for n in range(4):
        start_copy(n).wait()
    scale = lax.rsqrt(norm + EPS)
    xx_start = norm / (norm + EPS)
    pieces = []
    for j in range(nsrc):
        block = (start if j == 0 else start_halo[places[j - 1]]) * scale
        if j == 0:
            ts[...] = block
        pieces.append((block * alive[j]).astype(BF16))
    for ref in (xs, ys, us):
        ref[...] = nothing

    def share_halo(z, slot, halo):
        zsend[slot] = z.astype(HALO)

        @pl.when(halo)
        def _():
            for n in (2, 3, 0, 1):
                halo_copy(n, slot).start()

    def share_sums(x, t, y, z, slot):
        send_rows([inner(x, z), inner(t, z), inner(y, z), inner(z, z)], slot)

    def rotate(slot, first, a, xx, yy, tt, inv):
        xz, tz, yz, zz = wait_rows(slot, 4)
        off = 0.5 * ((yy - a * a) * inv + xz)
        gap = 0.5 * (a - tz)
        square = gap * gap + off * off
        over = jnp.where(square > 0, lax.rsqrt(jnp.where(square > 0, square, 1.0)), 0.0)
        energy = 0.5 * (a + tz) - square * over
        half = 0.5 + 0.5 * jnp.abs(gap) * over
        turn = lax.rsqrt(half)
        major = half * turn
        minor = 0.5 * jnp.abs(off) * over * turn
        cosine = jnp.where(gap <= 0, major, minor)
        sine = jnp.where(gap <= 0, minor, major) * jnp.where(off >= 0, -1.0, 1.0)
        if first:
            cosine, sine = jnp.zeros_like(gap), jnp.ones_like(gap)
        cc, cs, ss = cosine * cosine, cosine * sine, sine * sine
        xt = a * (1.0 - xx) * inv
        new_a = cc * a + 2.0 * cs * off + ss * tz
        new_yy = cc * yy + 2.0 * cs * yz + ss * zz
        new_xx = cc * xx + 2.0 * cs * xt + ss * tt
        rho = jnp.maximum(new_yy - 2.0 * new_a * new_a + new_a * new_a * new_xx, 0.0)
        new_inv = lax.rsqrt(rho + EPS)
        return energy, cosine, sine, new_a, new_xx, new_yy, rho / (rho + EPS), new_inv

    image = shared_multiply(0, nothing, pieces)
    zs[...] = image
    share_halo(image, 0, True)
    share_sums(xs[...], ts[...], ys[...], image, 0)

    def round_of(slot, first, last, carry, apply):
        total = multiply(nothing, env, renv, [(0, zsend[slot])])
        for n in range(4):
            halo_copy(n, slot).wait_recv()
        pieces = [None]
        for j in range(1, nsrc):
            pieces.append((zhalo[slot][places[j - 1]].astype(F32) * alive[j]).astype(BF16))
        w, turned = apply(total, pieces, lambda: rotate(slot, first, *carry))
        _, cosine, sine, a, xx, yy, tt, inv = turned
        y = cosine * ys[...] + sine * zs[...]
        u = cosine * us[...] + sine * w
        z = (u - a * y) * inv
        share_halo(z, 1 - slot, jnp.logical_not(last))
        x = cosine * xs[...] + sine * ts[...]
        t = (y - a * x) * inv
        share_sums(x, t, y, z, 1 - slot)
        xs[...] = x
        ys[...] = y
        us[...] = u
        ts[...] = t
        zs[...] = z
        for n in range(4):
            halo_copy(n, slot).wait_send()
        wait_rows_sent(slot)
        return a, xx, yy, tt, inv

    zero = jnp.zeros((1, 1), F32)
    carry = (zero, zero, zero, xx_start, zero + 1.0)
    carry = round_of(0, True, False, carry, lambda total, pieces, sums: (shared_multiply(1, total, pieces), sums()))
    carry = round_of(1, False, False, carry, lambda total, pieces, sums: local_multiply(total, pieces, sums, True))

    def two_rounds(k, carry):
        for slot in range(2):
            last = jnp.logical_and(slot == 1, k == ITERS // 2 - 2)
            carry = round_of(slot, False, last, carry, lambda total, pieces, sums: local_multiply(total, pieces, sums, False))
        return carry

    carry = lax.fori_loop(0, ITERS // 2 - 1, two_rounds, carry)
    slot = ITERS % 2
    energy, cosine, sine, *_ = rotate(slot, False, *carry)
    state_ref[...] = cosine * xs[...] + sine * ts[...]
    energy_ref[0] = energy[0, 0]
    wait_rows_sent(slot)

    @pl.when(jnp.logical_not(last_site))
    def _():
        for i in range(len(steps)):
            env_copy(i).wait_send()
        for n in range(2):
            part_copy(n).wait_send()

    @pl.when(jnp.logical_not(first_site))
    def _():
        for g in range(groups):
            help_copy(g).wait_send()
        for n in range(2):
            piece_copy(n).wait_send()


def per_device(initial_state, left_env, edge_env, right_env, source_blocks, live_terms):
    nsrc, terms, width = left_env.shape[2], left_env.shape[3], left_env.shape[4]
    blocks, sites = lax.axis_size("sector"), lax.axis_size("site")
    count = (nsrc // 2) * (terms // GROUP)
    flat = (nsrc, terms * width, width)
    vmem = pl.BlockSpec(memory_space=pltpu.VMEM)
    smem = pl.BlockSpec(memory_space=pltpu.SMEM)
    anywhere = pl.BlockSpec(memory_space=pl.ANY)
    dma = pltpu.SemaphoreType.DMA
    body = functools.partial(kernel, blocks, float(blocks * width * width), sites, nsrc, terms)
    state, energy = pl.pallas_call(
        body,
        out_shape=(
            jax.ShapeDtypeStruct((width, width), F32),
            jax.ShapeDtypeStruct((1,), F32),
        ),
        in_specs=[anywhere, anywhere, anywhere, anywhere, smem, smem],
        out_specs=(vmem, smem),
        scratch_shapes=[
            pltpu.VMEM(flat, BF16),
            pltpu.VMEM(flat, BF16),
            pltpu.VMEM((2, *flat[1:]), BF16),
            pltpu.VMEM((2, *flat[1:]), BF16),
            pltpu.VMEM((width, width), F32),
            pltpu.VMEM((width, width), F32),
            pltpu.VMEM((width, width), F32),
            pltpu.VMEM((width, width), F32),
            pltpu.VMEM((width, width), F32),
            pltpu.VMEM((4, width, width), F32),
            pltpu.VMEM((2, width, width), HALO),
            pltpu.VMEM((4, width, width), HALO),
            pltpu.VMEM((4, width, width), HALO),
            pltpu.VMEM((2, 1, width), F32),
            pltpu.VMEM((2, blocks, 1, width), F32),
            pltpu.VMEM((2, 1, width), F32),
            pltpu.VMEM((2, 2 * GRID, 1, width), F32),
            pltpu.VMEM((2, 2, width, width), BF16),
            pltpu.VMEM((2, 2, width, width), BF16),
            pltpu.VMEM((2, width, width), PART),
            pltpu.VMEM((2, width, width), PART),
            dma((count,)), dma((count,)), dma((count,)), dma, dma((4,)), dma((4,)),
            dma((2, 4)), dma((2, 4)), dma((2,)), dma((2,)), dma((2,)), dma((2,)),
            dma, dma((count // 2,)), dma((count // 2,)), dma((2,)), dma((2,)), dma((2,)), dma((2,)),
        ],
        compiler_params=pltpu.CompilerParams(
            collective_id=0, has_side_effects=True, vmem_limit_bytes=60 * 1024 * 1024
        ),
        name="window",
    )(
        initial_state[0, 0],
        left_env.reshape(flat),
        edge_env.reshape(flat),
        right_env.reshape(flat),
        source_blocks.reshape(nsrc),
        live_terms.reshape(1),
    )
    return state[None, None], energy


def solution(mesh):
    placed = (
        P("site", "sector", None, None),
        P("site", "sector", None, None, None, None),
        P("sector", None, None, None, None),
        P("site", "sector", None, None, None, None),
        P("site", "sector", None),
        P("site", "sector"),
    )
    return jax.shard_map(
        per_device,
        mesh=mesh,
        in_specs=placed,
        out_specs=(P("site", "sector", None, None), P("site")),
        check_vma=False,
    )
```

```python
import functools

import jax
import jax.numpy as jnp
from jax import lax
from jax.experimental import pallas as pl
from jax.experimental.pallas import tpu as pltpu
from jax.sharding import PartitionSpec as P

GRID = 4
ITERS = 8
GROUP = 2
LATE_FIRST = 4
HALO = jnp.bfloat16
PART = jnp.bfloat16
EPS = 1e-06
MESH = pl.DeviceIdType.MESH
F32 = jnp.float32
BF16 = jnp.bfloat16


def kernel(
    blocks, cells, sites, nsrc, terms,
    start_ref, left_ref, edge_ref, right_ref, ids_ref, live_ref,
    state_ref, energy_ref,
    env, renv, help_env, help_renv, xs, ys, us, ts, zs, start_halo, zsend, zhalo_even, zhalo_odd, row_send, rows, norm_send, norms,
    piece_send, piece_in, part_send, part_in, facts_send, facts_in, help_halo,
    env_send, env_recv, renv_sem, start_sem, start_send, start_recv,
    halo_send, halo_recv, row_send_sem, row_recv_sem, norm_send_sem, norm_recv_sem,
    help_env_sem, help_renv_send, help_renv_recv, piece_sends, piece_recvs, part_sends, part_recvs,
    facts_sems, help_sends, help_recvs,
):
    site = lax.axis_index("site")
    me = lax.axis_index("sector")
    width = start_ref.shape[-1]
    groups = terms // GROUP
    steps = [(p, g) for p in range(nsrc // 2) for g in range(groups)]
    early = [i for i, (p, _) in enumerate(steps) if p == 0]
    late = [i for i, (p, _) in enumerate(steps) if p == 1]
    first_site, last_site = site == 0, site == sites - 1

    def peer(by):
        return lax.rem(me + by + blocks, blocks)

    barrier = pltpu.get_barrier_semaphore()

    @pl.when(site > 0)
    def _():
        pl.semaphore_signal(barrier, inc=1, device_id={"site": site - 1}, device_id_type=MESH)

    @pl.when(site < sites - 1)
    def _():
        pl.semaphore_signal(barrier, inc=1, device_id={"site": site + 1}, device_id_type=MESH)

    side = 2 * GRID
    base, spot, line = me - lax.rem(me, side), lax.rem(me, side), me // side
    planes = ([base + lax.rem(spot + d, side) for d in range(1, side)], [peer(d) for d in range(side, blocks, side)])
    for other in planes[0] + planes[1]:
        pl.semaphore_signal(barrier, inc=1, device_id={"sector": other}, device_id_type=MESH)

    def span(ref, p, g):
        return ref.at[pl.ds(2 * p, 2), pl.ds(g * GROUP * width, GROUP * width), :]

    pltpu.make_async_copy(start_ref, zs, start_sem).start()
    for i, (p, g) in enumerate(steps):
        pltpu.make_async_copy(span(right_ref, p, g), span(renv, p, g), renv_sem.at[i]).start()

    @pl.when(first_site)
    def _():
        for i, (p, g) in enumerate(steps):
            pltpu.make_async_copy(span(edge_ref, p, g), span(env, p, g), env_recv.at[i]).start()

    @pl.when(jnp.logical_not(last_site))
    def _():
        pltpu.make_async_copy(left_ref.at[pl.ds(2, 2)], help_env, help_env_sem).start()

    pl.semaphore_wait(
        barrier, len(planes[0]) + len(planes[1]) + jnp.where(site > 0, 1, 0) + jnp.where(site < sites - 1, 1, 0)
    )

    hops = (1, -1, GRID, -GRID)

    def env_copy(i):
        p, g = steps[i]
        return pltpu.make_async_remote_copy(
            src_ref=span(left_ref, p, g), dst_ref=span(env, p, g),
            send_sem=env_send.at[i], recv_sem=env_recv.at[i],
            device_id={"site": site + 1}, device_id_type=MESH,
        )

    def help_copy(g):
        return pltpu.make_async_remote_copy(
            src_ref=span(right_ref, 1, g), dst_ref=span(help_renv, 0, g),
            send_sem=help_renv_send.at[g], recv_sem=help_renv_recv.at[g],
            device_id={"site": site - 1}, device_id_type=MESH,
        )

    def facts_copy():
        return pltpu.make_async_remote_copy(
            src_ref=facts_send, dst_ref=facts_in, send_sem=facts_sems.at[0], recv_sem=facts_sems.at[1],
            device_id={"site": site - 1}, device_id_type=MESH,
        )

    def help_halo_copy(n):
        return pltpu.make_async_remote_copy(
            src_ref=zsend.at[0], dst_ref=help_halo.at[n],
            send_sem=help_sends.at[n], recv_sem=help_recvs.at[n],
            device_id={"site": site - 1, "sector": peer(hops[n])}, device_id_type=MESH,
        )

    def piece_copy(n):
        return pltpu.make_async_remote_copy(
            src_ref=piece_send.at[n], dst_ref=piece_in.at[n],
            send_sem=piece_sends.at[n], recv_sem=piece_recvs.at[n],
            device_id={"site": site - 1}, device_id_type=MESH,
        )

    def part_copy(n):
        return pltpu.make_async_remote_copy(
            src_ref=part_send.at[n], dst_ref=part_in.at[n],
            send_sem=part_sends.at[n], recv_sem=part_recvs.at[n],
            device_id={"site": site + 1}, device_id_type=MESH,
        )

    @pl.when(jnp.logical_not(last_site))
    def _():
        for i in early:
            env_copy(i).start()

    lane = lax.broadcasted_iota(jnp.int32, (1, width), 1)
    facts = jnp.where(lane == 0, live_ref[0, 0], 0)
    for j in range(1, nsrc):
        facts = jnp.where(lane == j, ids_ref[0, 0, j], facts)
    facts_send[...] = facts

    @pl.when(jnp.logical_not(first_site))
    def _():
        facts_copy().start()
        for g in range(groups - 1):
            help_copy(g).start()

    zhalo = (zhalo_even, zhalo_odd)

    def start_copy(n):
        return pltpu.make_async_remote_copy(
            src_ref=start_ref, dst_ref=start_halo.at[n],
            send_sem=start_send.at[n], recv_sem=start_recv.at[n],
            device_id={"sector": peer(hops[n])}, device_id_type=MESH,
        )

    def halo_copy(n, slot):
        return pltpu.make_async_remote_copy(
            src_ref=zsend.at[slot], dst_ref=zhalo[slot].at[n],
            send_sem=halo_send.at[slot, n], recv_sem=halo_recv.at[slot, n],
            device_id={"sector": peer(hops[n])}, device_id_type=MESH,
        )

    far_first = sorted(range(1, blocks), key=lambda d: abs(d - blocks // 2))

    def send_rows(values, slot):
        lane = lax.broadcasted_iota(jnp.int32, (1, width), 1)
        row = jnp.zeros((1, width), F32)
        for n, value in enumerate(values):
            row = jnp.where(lane == n, value, row)
        row_send[slot] = row
        rows[slot, me] = row
        for d in far_first:
            pltpu.make_async_remote_copy(
                src_ref=row_send.at[slot], dst_ref=rows.at[slot, me],
                send_sem=row_send_sem.at[slot], recv_sem=row_recv_sem.at[slot],
                device_id={"sector": peer(d)}, device_id_type=MESH,
            ).start()

    def wait_rows(slot, count):
        pltpu.make_async_copy(
            rows.at[slot, pl.ds(0, blocks - 1)], rows.at[slot, pl.ds(0, blocks - 1)], row_recv_sem.at[slot]
        ).wait()
        total = jnp.sum(rows[slot], axis=0)
        return [total[:, n:n + 1] / cells for n in range(count)]

    def wait_rows_sent(slot):
        pltpu.make_async_copy(
            rows.at[slot, pl.ds(0, blocks - 1)], rows.at[slot, pl.ds(0, blocks - 1)], row_send_sem.at[slot]
        ).wait()

    def inner(a, b):
        return jnp.sum(jnp.sum(a * b, axis=0, keepdims=True), axis=1, keepdims=True)

    def place_of(source):
        offset = source - me
        return jnp.where(offset == -1, 0, jnp.where(offset == 1, 1, jnp.where(offset == -GRID, 2, 3)))

    places = [place_of(ids_ref[0, 0, j]) for j in range(1, nsrc)]
    alive = [(j < live_ref[0, 0]).astype(F32) for j in range(nsrc)]

    def multiply(total, e_ref, r_ref, jobs, wait=None):
        size = GROUP if wait else terms
        for g in range(terms // size):
            if wait:
                wait(g)
            at = slice(g * size * width, (g + 1) * size * width)
            products = [
                jnp.dot(e_ref[j, at, :], piece, preferred_element_type=F32).astype(BF16) for j, piece in jobs
            ]
            for product, (j, _) in zip(products, jobs):
                lhs = jnp.concatenate([product[w * width:(w + 1) * width] for w in range(size)], axis=1)
                total = total + jnp.dot(lhs, r_ref[j, at, :], preferred_element_type=F32)
        return total

    def wait_env(i):
        pltpu.make_async_copy(span(env, *steps[i]), span(env, *steps[i]), env_recv.at[i]).wait()

    nothing = jnp.zeros((width, width), F32)

    def shared_multiply(n, total, pieces, sums):
        if n == 0:
            piece_send[0, 0] = pieces[2]
            piece_send[0, 1] = pieces[3]

            @pl.when(jnp.logical_not(first_site))
            def _():
                piece_copy(0).start()
                help_copy(groups - 1).start()

        @pl.when(jnp.logical_not(last_site))
        def _():
            if n == 0:
                pltpu.make_async_copy(piece_in.at[0], piece_in.at[0], piece_recvs.at[0]).wait()
                pltpu.make_async_copy(help_env, help_env, help_env_sem).wait()
                pltpu.make_async_copy(facts_in, facts_in, facts_sems.at[1]).wait()
                two = [piece_in[0, 0], piece_in[0, 1]]
            else:
                for m in range(4):
                    pltpu.make_async_copy(help_halo.at[m], help_halo.at[m], help_recvs.at[m]).wait()
                facts = facts_in[...]
                two = []
                for j in range(2, nsrc):
                    piece = help_halo[place_of(facts[0, j])].astype(F32)
                    two.append((piece * (j < facts[0, 0]).astype(F32)).astype(BF16))

            def arrived(g):
                pltpu.make_async_copy(
                    span(help_renv, 0, g), span(help_renv, 0, g), help_renv_recv.at[g]
                ).wait()

            part_send[n] = multiply(
                nothing, help_env, help_renv, [(0, two[0]), (1, two[1])], None if n else arrived
            ).astype(PART)
            part_copy(n).start()
            for i in (late[:LATE_FIRST], late[LATE_FIRST:])[n]:
                env_copy(i).start()

        if n == 0:
            for i, (p, g) in enumerate(steps):
                pltpu.make_async_copy(span(renv, p, g), span(renv, p, g), renv_sem.at[i]).wait()
        if n == 0:
            total = multiply(total, env, renv, [(0, pieces[0]), (1, pieces[1])], lambda g: wait_env(early[g]))
        else:
            total = multiply(total, env, renv, [(1, pieces[1])])
        turned = sums()

        @pl.when(first_site)
        def _():
            if n == 0:
                for i in late:
                    wait_env(i)
            part_in[n] = multiply(nothing, env, renv, [(2, pieces[2]), (3, pieces[3])]).astype(PART)

        @pl.when(jnp.logical_not(first_site))
        def _():
            pltpu.make_async_copy(part_in.at[n], part_in.at[n], part_recvs.at[n]).wait()

        return total + part_in[n].astype(F32), turned

    def local_multiply(total, pieces, sums, wait):
        if wait:
            @pl.when(jnp.logical_not(first_site))
            def _():
                for i in late:
                    wait_env(i)
        total = multiply(total, env, renv, [(1, pieces[1])])
        turned = sums()
        return multiply(total, env, renv, [(j, pieces[j]) for j in range(2, nsrc)]), turned

    pltpu.make_async_copy(start_ref, zs, start_sem).wait()
    start = zs[...]
    norm = inner(start, start)
    for stage, (others, own) in enumerate(zip(planes, (spot, line))):
        row = jnp.broadcast_to(norm, (1, width))
        count = len(others)
        norm_send[stage] = row
        norms[stage, own] = row
        for other in others:
            pltpu.make_async_remote_copy(
                src_ref=norm_send.at[stage], dst_ref=norms.at[stage, own],
                send_sem=norm_send_sem.at[stage], recv_sem=norm_recv_sem.at[stage],
                device_id={"sector": other}, device_id_type=MESH,
            ).start()
        came = norms.at[stage, pl.ds(0, count)]
        pltpu.make_async_copy(came, came, norm_recv_sem.at[stage]).wait()
        norm = jnp.sum(norms[stage, 0:count + 1], axis=0)[:, 0:1]
        pltpu.make_async_copy(came, came, norm_send_sem.at[stage]).wait()
    norm = norm / cells
    for n in range(4):
        start_copy(n).start()
    for n in range(4):
        start_copy(n).wait()
    scale = lax.rsqrt(norm + EPS)
    xx_start = norm / (norm + EPS)
    pieces = []
    for j in range(nsrc):
        block = (start if j == 0 else start_halo[places[j - 1]]) * scale
        if j == 0:
            ts[...] = block
        pieces.append((block * alive[j]).astype(BF16))
    for ref in (xs, ys, us):
        ref[...] = nothing

    def share_halo(z, slot, halo):
        zsend[slot] = z.astype(HALO)

        @pl.when(halo)
        def _():
            for n in (2, 3, 0, 1):
                halo_copy(n, slot).start()

    def share_sums(x, t, y, z, slot):
        send_rows([inner(x, z), inner(t, z), inner(y, z), inner(z, z)], slot)

    def rotate(slot, first, a, xx, yy, tt, inv):
        xz, tz, yz, zz = wait_rows(slot, 4)
        off = 0.5 * ((yy - a * a) * inv + xz)
        gap = 0.5 * (a - tz)
        square = gap * gap + off * off
        over = jnp.where(square > 0, lax.rsqrt(jnp.where(square > 0, square, 1.0)), 0.0)
        energy = 0.5 * (a + tz) - square * over
        half = 0.5 + 0.5 * jnp.abs(gap) * over
        turn = lax.rsqrt(half)
        major = half * turn
        minor = 0.5 * jnp.abs(off) * over * turn
        cosine = jnp.where(gap <= 0, major, minor)
        sine = jnp.where(gap <= 0, minor, major) * jnp.where(off >= 0, -1.0, 1.0)
        if first:
            cosine, sine = jnp.zeros_like(gap), jnp.ones_like(gap)
        cc, cs, ss = cosine * cosine, cosine * sine, sine * sine
        xt = a * (1.0 - xx) * inv
        new_a = cc * a + 2.0 * cs * off + ss * tz
        new_yy = cc * yy + 2.0 * cs * yz + ss * zz
        new_xx = cc * xx + 2.0 * cs * xt + ss * tt
        rho = jnp.maximum(new_yy - 2.0 * new_a * new_a + new_a * new_a * new_xx, 0.0)
        new_inv = lax.rsqrt(rho + EPS)
        return energy, cosine, sine, new_a, new_xx, new_yy, rho / (rho + EPS), new_inv

    image, _ = shared_multiply(0, nothing, pieces, lambda: None)
    zs[...] = image
    share_halo(image, 0, True)

    @pl.when(jnp.logical_not(first_site))
    def _():
        for n in (2, 3, 0, 1):
            help_halo_copy(n).start()

    share_sums(xs[...], ts[...], ys[...], image, 0)

    def round_of(slot, first, last, carry, apply):
        total = multiply(nothing, env, renv, [(0, zsend[slot])])
        for n in range(4):
            halo_copy(n, slot).wait_recv()
        pieces = [None]
        for j in range(1, nsrc):
            pieces.append((zhalo[slot][places[j - 1]].astype(F32) * alive[j]).astype(BF16))
        w, turned = apply(total, pieces, lambda: rotate(slot, first, *carry))
        _, cosine, sine, a, xx, yy, tt, inv = turned
        y = cosine * ys[...] + sine * zs[...]
        u = cosine * us[...] + sine * w
        z = (u - a * y) * inv
        share_halo(z, 1 - slot, jnp.logical_not(last))
        x = cosine * xs[...] + sine * ts[...]
        t = (y - a * x) * inv
        share_sums(x, t, y, z, 1 - slot)
        xs[...] = x
        ys[...] = y
        us[...] = u
        ts[...] = t
        zs[...] = z
        for n in range(4):
            halo_copy(n, slot).wait_send()
        wait_rows_sent(slot)
        if first:
            @pl.when(jnp.logical_not(first_site))
            def _():
                for n in range(4):
                    help_halo_copy(n).wait_send()

        return a, xx, yy, tt, inv

    zero = jnp.zeros((1, 1), F32)
    carry = (zero, zero, zero, xx_start, zero + 1.0)
    carry = round_of(0, True, False, carry, lambda total, pieces, sums: shared_multiply(1, total, pieces, sums))
    carry = round_of(1, False, False, carry, lambda total, pieces, sums: local_multiply(total, pieces, sums, True))

    def two_rounds(k, carry):
        for slot in range(2):
            last = jnp.logical_and(slot == 1, k == ITERS // 2 - 2)
            carry = round_of(slot, False, last, carry, lambda total, pieces, sums: local_multiply(total, pieces, sums, False))
        return carry

    carry = lax.fori_loop(0, ITERS // 2 - 1, two_rounds, carry)
    slot = ITERS % 2
    energy, cosine, sine, *_ = rotate(slot, False, *carry)
    state_ref[...] = cosine * xs[...] + sine * ts[...]
    energy_ref[0] = energy[0, 0]
    wait_rows_sent(slot)

    @pl.when(jnp.logical_not(last_site))
    def _():
        for i in range(len(steps)):
            env_copy(i).wait_send()
        for n in range(2):
            part_copy(n).wait_send()

    @pl.when(jnp.logical_not(first_site))
    def _():
        for g in range(groups):
            help_copy(g).wait_send()
        piece_copy(0).wait_send()
        facts_copy().wait_send()


def per_device(initial_state, left_env, edge_env, right_env, source_blocks, live_terms):
    nsrc, terms, width = left_env.shape[2], left_env.shape[3], left_env.shape[4]
    blocks, sites = lax.axis_size("sector"), lax.axis_size("site")
    count = (nsrc // 2) * (terms // GROUP)
    flat = (nsrc, terms * width, width)
    vmem = pl.BlockSpec(memory_space=pltpu.VMEM)
    smem = pl.BlockSpec(memory_space=pltpu.SMEM)
    anywhere = pl.BlockSpec(memory_space=pl.ANY)
    dma = pltpu.SemaphoreType.DMA
    body = functools.partial(kernel, blocks, float(blocks * width * width), sites, nsrc, terms)
    state, energy = pl.pallas_call(
        body,
        out_shape=(
            jax.ShapeDtypeStruct((width, width), F32),
            jax.ShapeDtypeStruct((1,), F32),
        ),
        in_specs=[anywhere, anywhere, anywhere, anywhere, smem, smem],
        out_specs=(vmem, smem),
        scratch_shapes=[
            pltpu.VMEM(flat, BF16),
            pltpu.VMEM(flat, BF16),
            pltpu.VMEM((2, *flat[1:]), BF16),
            pltpu.VMEM((2, *flat[1:]), BF16),
            pltpu.VMEM((width, width), F32),
            pltpu.VMEM((width, width), F32),
            pltpu.VMEM((width, width), F32),
            pltpu.VMEM((width, width), F32),
            pltpu.VMEM((width, width), F32),
            pltpu.VMEM((4, width, width), F32),
            pltpu.VMEM((2, width, width), HALO),
            pltpu.VMEM((4, width, width), HALO),
            pltpu.VMEM((4, width, width), HALO),
            pltpu.VMEM((2, 1, width), F32),
            pltpu.VMEM((2, blocks, 1, width), F32),
            pltpu.VMEM((2, 1, width), F32),
            pltpu.VMEM((2, 2 * GRID, 1, width), F32),
            pltpu.VMEM((1, 2, width, width), BF16),
            pltpu.VMEM((1, 2, width, width), BF16),
            pltpu.VMEM((2, width, width), PART),
            pltpu.VMEM((2, width, width), PART),
            pltpu.VMEM((1, width), jnp.int32),
            pltpu.VMEM((1, width), jnp.int32),
            pltpu.VMEM((4, width, width), HALO),
            dma((count,)), dma((count,)), dma((count,)), dma, dma((4,)), dma((4,)),
            dma((2, 4)), dma((2, 4)), dma((2,)), dma((2,)), dma((2,)), dma((2,)),
            dma, dma((count // 2,)), dma((count // 2,)), dma((2,)), dma((2,)), dma((2,)), dma((2,)),
            dma((2,)), dma((4,)), dma((4,)),
        ],
        compiler_params=pltpu.CompilerParams(
            collective_id=0, has_side_effects=True, vmem_limit_bytes=60 * 1024 * 1024
        ),
        name="window",
    )(
        initial_state[0, 0],
        left_env.reshape(flat),
        edge_env.reshape(flat),
        right_env.reshape(flat),
        source_blocks,
        live_terms,
    )
    return state[None, None], energy


def solution(mesh):
    placed = (
        P("site", "sector", None, None),
        P("site", "sector", None, None, None, None),
        P("sector", None, None, None, None),
        P("site", "sector", None, None, None, None),
        P("site", "sector", None),
        P("site", "sector"),
    )
    return jax.shard_map(
        per_device,
        mesh=mesh,
        in_specs=placed,
        out_specs=(P("site", "sector", None, None), P("site")),
        check_vma=False,
    )
```

```python
import functools

import jax
import jax.numpy as jnp
from jax import lax
from jax.experimental import pallas as pl
from jax.experimental.pallas import tpu as pltpu
from jax.sharding import PartitionSpec as P

GRID = 4
ITERS = 8
GROUP = 2
LATE_FIRST = 4
HALO = jnp.bfloat16
PART = jnp.bfloat16
EPS = 1e-06
MESH = pl.DeviceIdType.MESH
F32 = jnp.float32
BF16 = jnp.bfloat16


def kernel(
    blocks, cells, sites, nsrc, terms,
    start_ref, left_ref, edge_ref, right_ref, ids_ref, live_ref,
    state_ref, energy_ref,
    env, renv, help_env, help_renv, xs, ys, us, ts, zs, start_halo, zsend, zhalo_even, zhalo_odd, row_send, rows, norm_send, norms,
    piece_send, piece_in, part_send, part_in, facts_send, facts_in, help_halo,
    env_send, env_recv, renv_sem, start_sem, start_send, start_recv,
    halo_send, halo_recv, row_send_sem, row_recv_sem, norm_send_sem, norm_recv_sem,
    help_env_sem, help_renv_send, help_renv_recv, piece_sends, piece_recvs, part_sends, part_recvs,
    facts_sems, help_sends, help_recvs,
):
    site = lax.axis_index("site")
    me = lax.axis_index("sector")
    width = start_ref.shape[-1]
    groups = terms // GROUP
    steps = [(p, g) for p in range(nsrc // 2) for g in range(groups)]
    early = [i for i, (p, _) in enumerate(steps) if p == 0]
    late = [i for i, (p, _) in enumerate(steps) if p == 1]
    first_site, last_site = site == 0, site == sites - 1

    def peer(by):
        return lax.rem(me + by + blocks, blocks)

    barrier = pltpu.get_barrier_semaphore()

    @pl.when(site > 0)
    def _():
        pl.semaphore_signal(barrier, inc=1, device_id={"site": site - 1}, device_id_type=MESH)

    @pl.when(site < sites - 1)
    def _():
        pl.semaphore_signal(barrier, inc=1, device_id={"site": site + 1}, device_id_type=MESH)

    side = 2 * GRID
    spot, base = lax.rem(me, side), me - lax.rem(me, side)
    planes = (
        [me + 1 - 2 * lax.rem(me, 2)],
        [base + lax.rem(spot + d, side) for d in range(2, side, 2)],
        [peer(d) for d in range(side, blocks, side)],
    )
    owns = (lax.rem(me, 2), spot // 2, me // side)
    for other in planes[0] + planes[1] + planes[2]:
        pl.semaphore_signal(barrier, inc=1, device_id={"sector": other}, device_id_type=MESH)

    def span(ref, p, g):
        return ref.at[pl.ds(2 * p, 2), pl.ds(g * GROUP * width, GROUP * width), :]

    pltpu.make_async_copy(start_ref, zs, start_sem).start()
    for i, (p, g) in enumerate(steps):
        pltpu.make_async_copy(span(right_ref, p, g), span(renv, p, g), renv_sem.at[i]).start()

    @pl.when(first_site)
    def _():
        for i, (p, g) in enumerate(steps):
            pltpu.make_async_copy(span(edge_ref, p, g), span(env, p, g), env_recv.at[i]).start()

    @pl.when(jnp.logical_not(last_site))
    def _():
        pltpu.make_async_copy(left_ref.at[pl.ds(2, 2)], help_env, help_env_sem).start()

    pl.semaphore_wait(
        barrier, sum(len(plane) for plane in planes) + jnp.where(site > 0, 1, 0) + jnp.where(site < sites - 1, 1, 0)
    )

    hops = (1, -1, GRID, -GRID)

    def env_copy(i):
        p, g = steps[i]
        return pltpu.make_async_remote_copy(
            src_ref=span(left_ref, p, g), dst_ref=span(env, p, g),
            send_sem=env_send.at[i], recv_sem=env_recv.at[i],
            device_id={"site": site + 1}, device_id_type=MESH,
        )

    def help_copy(g):
        return pltpu.make_async_remote_copy(
            src_ref=span(right_ref, 1, g), dst_ref=span(help_renv, 0, g),
            send_sem=help_renv_send.at[g], recv_sem=help_renv_recv.at[g],
            device_id={"site": site - 1}, device_id_type=MESH,
        )

    def facts_copy():
        return pltpu.make_async_remote_copy(
            src_ref=facts_send, dst_ref=facts_in, send_sem=facts_sems.at[0], recv_sem=facts_sems.at[1],
            device_id={"site": site - 1}, device_id_type=MESH,
        )

    def help_halo_copy(n):
        return pltpu.make_async_remote_copy(
            src_ref=zsend.at[0], dst_ref=help_halo.at[n],
            send_sem=help_sends.at[n], recv_sem=help_recvs.at[n],
            device_id={"site": site - 1, "sector": peer(hops[n])}, device_id_type=MESH,
        )

    def piece_copy(n):
        return pltpu.make_async_remote_copy(
            src_ref=piece_send.at[n], dst_ref=piece_in.at[n],
            send_sem=piece_sends.at[n], recv_sem=piece_recvs.at[n],
            device_id={"site": site - 1}, device_id_type=MESH,
        )

    def part_copy(n):
        return pltpu.make_async_remote_copy(
            src_ref=part_send.at[n], dst_ref=part_in.at[n],
            send_sem=part_sends.at[n], recv_sem=part_recvs.at[n],
            device_id={"site": site + 1}, device_id_type=MESH,
        )

    @pl.when(jnp.logical_not(last_site))
    def _():
        for i in early:
            env_copy(i).start()

    lane = lax.broadcasted_iota(jnp.int32, (1, width), 1)
    facts = jnp.where(lane == 0, live_ref[0, 0], 0)
    for j in range(1, nsrc):
        facts = jnp.where(lane == j, ids_ref[0, 0, j], facts)
    facts_send[...] = facts

    @pl.when(jnp.logical_not(first_site))
    def _():
        facts_copy().start()
        for g in range(groups - 1):
            help_copy(g).start()

    zhalo = (zhalo_even, zhalo_odd)

    def start_copy(n):
        return pltpu.make_async_remote_copy(
            src_ref=start_ref, dst_ref=start_halo.at[n],
            send_sem=start_send.at[n], recv_sem=start_recv.at[n],
            device_id={"sector": peer(hops[n])}, device_id_type=MESH,
        )

    def halo_copy(n, slot):
        return pltpu.make_async_remote_copy(
            src_ref=zsend.at[slot], dst_ref=zhalo[slot].at[n],
            send_sem=halo_send.at[slot, n], recv_sem=halo_recv.at[slot, n],
            device_id={"sector": peer(hops[n])}, device_id_type=MESH,
        )

    far_first = sorted(range(1, blocks), key=lambda d: abs(d - blocks // 2))

    def send_rows(values, slot):
        lane = lax.broadcasted_iota(jnp.int32, (1, width), 1)
        row = jnp.zeros((1, width), F32)
        for n, value in enumerate(values):
            row = jnp.where(lane == n, value, row)
        row_send[slot] = row
        rows[slot, me] = row
        for d in far_first:
            pltpu.make_async_remote_copy(
                src_ref=row_send.at[slot], dst_ref=rows.at[slot, me],
                send_sem=row_send_sem.at[slot], recv_sem=row_recv_sem.at[slot],
                device_id={"sector": peer(d)}, device_id_type=MESH,
            ).start()

    def wait_rows(slot, count):
        pltpu.make_async_copy(
            rows.at[slot, pl.ds(0, blocks - 1)], rows.at[slot, pl.ds(0, blocks - 1)], row_recv_sem.at[slot]
        ).wait()
        total = jnp.sum(rows[slot], axis=0)
        return [total[:, n:n + 1] / cells for n in range(count)]

    def wait_rows_sent(slot):
        pltpu.make_async_copy(
            rows.at[slot, pl.ds(0, blocks - 1)], rows.at[slot, pl.ds(0, blocks - 1)], row_send_sem.at[slot]
        ).wait()

    def inner(a, b):
        return jnp.sum(jnp.sum(a * b, axis=0, keepdims=True), axis=1, keepdims=True)

    def place_of(source):
        offset = source - me
        return jnp.where(offset == -1, 0, jnp.where(offset == 1, 1, jnp.where(offset == -GRID, 2, 3)))

    places = [place_of(ids_ref[0, 0, j]) for j in range(1, nsrc)]
    alive = [(j < live_ref[0, 0]).astype(F32) for j in range(nsrc)]

    def multiply(total, e_ref, r_ref, jobs, wait=None):
        size = GROUP if wait else terms
        for g in range(terms // size):
            if wait:
                wait(g)
            at = slice(g * size * width, (g + 1) * size * width)
            products = [
                jnp.dot(e_ref[j, at, :], piece, preferred_element_type=F32).astype(BF16) for j, piece in jobs
            ]
            for product, (j, _) in zip(products, jobs):
                lhs = jnp.concatenate([product[w * width:(w + 1) * width] for w in range(size)], axis=1)
                total = total + jnp.dot(lhs, r_ref[j, at, :], preferred_element_type=F32)
        return total

    def wait_env(i):
        pltpu.make_async_copy(span(env, *steps[i]), span(env, *steps[i]), env_recv.at[i]).wait()

    nothing = jnp.zeros((width, width), F32)

    def shared_multiply(n, total, pieces, sums):
        if n == 0:
            piece_send[0, 0] = pieces[2]
            piece_send[0, 1] = pieces[3]

            @pl.when(jnp.logical_not(first_site))
            def _():
                piece_copy(0).start()
                help_copy(groups - 1).start()

        @pl.when(jnp.logical_not(last_site))
        def _():
            if n == 0:
                pltpu.make_async_copy(piece_in.at[0], piece_in.at[0], piece_recvs.at[0]).wait()
                pltpu.make_async_copy(help_env, help_env, help_env_sem).wait()
                pltpu.make_async_copy(facts_in, facts_in, facts_sems.at[1]).wait()
                two = [piece_in[0, 0], piece_in[0, 1]]
            else:
                for m in range(4):
                    pltpu.make_async_copy(help_halo.at[m], help_halo.at[m], help_recvs.at[m]).wait()
                facts = facts_in[...]
                two = []
                for j in range(2, nsrc):
                    piece = help_halo[place_of(facts[0, j])].astype(F32)
                    two.append((piece * (j < facts[0, 0]).astype(F32)).astype(BF16))

            def arrived(g):
                pltpu.make_async_copy(
                    span(help_renv, 0, g), span(help_renv, 0, g), help_renv_recv.at[g]
                ).wait()

            part_send[n] = multiply(
                nothing, help_env, help_renv, [(0, two[0]), (1, two[1])], None if n else arrived
            ).astype(PART)
            part_copy(n).start()
            for i in (late[:LATE_FIRST], late[LATE_FIRST:])[n]:
                env_copy(i).start()

        if n == 0:
            for i, (p, g) in enumerate(steps):
                pltpu.make_async_copy(span(renv, p, g), span(renv, p, g), renv_sem.at[i]).wait()
        if n == 0:
            total = multiply(total, env, renv, [(0, pieces[0]), (1, pieces[1])], lambda g: wait_env(early[g]))
        else:
            total = multiply(total, env, renv, [(1, pieces[1])])
        turned = sums()

        @pl.when(first_site)
        def _():
            if n == 0:
                for i in late:
                    wait_env(i)
            part_in[n] = multiply(nothing, env, renv, [(2, pieces[2]), (3, pieces[3])]).astype(PART)

        @pl.when(jnp.logical_not(first_site))
        def _():
            pltpu.make_async_copy(part_in.at[n], part_in.at[n], part_recvs.at[n]).wait()

        return total + part_in[n].astype(F32), turned

    def local_multiply(total, pieces, sums, wait):
        if wait:
            @pl.when(jnp.logical_not(first_site))
            def _():
                for i in late:
                    wait_env(i)
        total = multiply(total, env, renv, [(1, pieces[1])])
        turned = sums()
        return multiply(total, env, renv, [(j, pieces[j]) for j in range(2, nsrc)]), turned

    pltpu.make_async_copy(start_ref, zs, start_sem).wait()
    start = zs[...]
    norm = inner(start, start)
    for stage, (others, own) in enumerate(zip(planes, owns)):
        row = jnp.broadcast_to(norm, (1, width))
        count = len(others)
        norm_send[stage] = row
        norms[stage, own] = row
        for other in others:
            pltpu.make_async_remote_copy(
                src_ref=norm_send.at[stage], dst_ref=norms.at[stage, own],
                send_sem=norm_send_sem.at[stage], recv_sem=norm_recv_sem.at[stage],
                device_id={"sector": other}, device_id_type=MESH,
            ).start()
        came = norms.at[stage, pl.ds(0, count)]
        pltpu.make_async_copy(came, came, norm_recv_sem.at[stage]).wait()
        norm = jnp.sum(norms[stage, 0:count + 1], axis=0)[:, 0:1]
        pltpu.make_async_copy(came, came, norm_send_sem.at[stage]).wait()
    norm = norm / cells
    for n in range(4):
        start_copy(n).start()
    for n in range(4):
        start_copy(n).wait()
    scale = lax.rsqrt(norm + EPS)
    xx_start = norm / (norm + EPS)
    pieces = []
    for j in range(nsrc):
        block = (start if j == 0 else start_halo[places[j - 1]]) * scale
        if j == 0:
            ts[...] = block
        pieces.append((block * alive[j]).astype(BF16))
    for ref in (xs, ys, us):
        ref[...] = nothing

    def share_halo(z, slot, halo):
        zsend[slot] = z.astype(HALO)

        @pl.when(halo)
        def _():
            for n in (2, 3, 0, 1):
                halo_copy(n, slot).start()

    def share_sums(x, t, y, z, slot):
        send_rows([inner(x, z), inner(t, z), inner(y, z), inner(z, z)], slot)

    def rotate(slot, first, a, xx, yy, tt, inv):
        xz, tz, yz, zz = wait_rows(slot, 4)
        off = 0.5 * ((yy - a * a) * inv + xz)
        gap = 0.5 * (a - tz)
        square = gap * gap + off * off
        over = jnp.where(square > 0, lax.rsqrt(jnp.where(square > 0, square, 1.0)), 0.0)
        energy = 0.5 * (a + tz) - square * over
        half = 0.5 + 0.5 * jnp.abs(gap) * over
        turn = lax.rsqrt(half)
        major = half * turn
        minor = 0.5 * jnp.abs(off) * over * turn
        cosine = jnp.where(gap <= 0, major, minor)
        sine = jnp.where(gap <= 0, minor, major) * jnp.where(off >= 0, -1.0, 1.0)
        if first:
            cosine, sine = jnp.zeros_like(gap), jnp.ones_like(gap)
        cc, cs, ss = cosine * cosine, cosine * sine, sine * sine
        xt = a * (1.0 - xx) * inv
        new_a = cc * a + 2.0 * cs * off + ss * tz
        new_yy = cc * yy + 2.0 * cs * yz + ss * zz
        new_xx = cc * xx + 2.0 * cs * xt + ss * tt
        rho = jnp.maximum(new_yy - 2.0 * new_a * new_a + new_a * new_a * new_xx, 0.0)
        new_inv = lax.rsqrt(rho + EPS)
        return energy, cosine, sine, new_a, new_xx, new_yy, rho / (rho + EPS), new_inv

    image, _ = shared_multiply(0, nothing, pieces, lambda: None)
    zs[...] = image
    share_halo(image, 0, True)

    @pl.when(jnp.logical_not(first_site))
    def _():
        for n in (2, 3, 0, 1):
            help_halo_copy(n).start()

    share_sums(xs[...], ts[...], ys[...], image, 0)

    def round_of(slot, first, last, carry, apply):
        total = multiply(nothing, env, renv, [(0, zsend[slot])])
        for n in range(4):
            halo_copy(n, slot).wait_recv()
        pieces = [None]
        for j in range(1, nsrc):
            pieces.append((zhalo[slot][places[j - 1]].astype(F32) * alive[j]).astype(BF16))
        w, turned = apply(total, pieces, lambda: rotate(slot, first, *carry))
        _, cosine, sine, a, xx, yy, tt, inv = turned
        y = cosine * ys[...] + sine * zs[...]
        u = cosine * us[...] + sine * w
        z = (u - a * y) * inv
        share_halo(z, 1 - slot, jnp.logical_not(last))
        x = cosine * xs[...] + sine * ts[...]
        t = (y - a * x) * inv
        share_sums(x, t, y, z, 1 - slot)
        xs[...] = x
        ys[...] = y
        us[...] = u
        ts[...] = t
        zs[...] = z
        for n in range(4):
            halo_copy(n, slot).wait_send()
        wait_rows_sent(slot)
        if first:
            @pl.when(jnp.logical_not(first_site))
            def _():
                for n in range(4):
                    help_halo_copy(n).wait_send()

        return a, xx, yy, tt, inv

    zero = jnp.zeros((1, 1), F32)
    carry = (zero, zero, zero, xx_start, zero + 1.0)
    carry = round_of(0, True, False, carry, lambda total, pieces, sums: shared_multiply(1, total, pieces, sums))
    carry = round_of(1, False, False, carry, lambda total, pieces, sums: local_multiply(total, pieces, sums, True))

    def two_rounds(k, carry):
        for slot in range(2):
            last = jnp.logical_and(slot == 1, k == ITERS // 2 - 2)
            carry = round_of(slot, False, last, carry, lambda total, pieces, sums: local_multiply(total, pieces, sums, False))
        return carry

    carry = lax.fori_loop(0, ITERS // 2 - 1, two_rounds, carry)
    slot = ITERS % 2
    energy, cosine, sine, *_ = rotate(slot, False, *carry)
    state_ref[...] = cosine * xs[...] + sine * ts[...]
    energy_ref[0] = energy[0, 0]
    wait_rows_sent(slot)

    @pl.when(jnp.logical_not(last_site))
    def _():
        for i in range(len(steps)):
            env_copy(i).wait_send()
        for n in range(2):
            part_copy(n).wait_send()

    @pl.when(jnp.logical_not(first_site))
    def _():
        for g in range(groups):
            help_copy(g).wait_send()
        piece_copy(0).wait_send()
        facts_copy().wait_send()


def per_device(initial_state, left_env, edge_env, right_env, source_blocks, live_terms):
    nsrc, terms, width = left_env.shape[2], left_env.shape[3], left_env.shape[4]
    blocks, sites = lax.axis_size("sector"), lax.axis_size("site")
    count = (nsrc // 2) * (terms // GROUP)
    flat = (nsrc, terms * width, width)
    vmem = pl.BlockSpec(memory_space=pltpu.VMEM)
    smem = pl.BlockSpec(memory_space=pltpu.SMEM)
    anywhere = pl.BlockSpec(memory_space=pl.ANY)
    dma = pltpu.SemaphoreType.DMA
    body = functools.partial(kernel, blocks, float(blocks * width * width), sites, nsrc, terms)
    state, energy = pl.pallas_call(
        body,
        out_shape=(
            jax.ShapeDtypeStruct((width, width), F32),
            jax.ShapeDtypeStruct((1,), F32),
        ),
        in_specs=[anywhere, anywhere, anywhere, anywhere, smem, smem],
        out_specs=(vmem, smem),
        scratch_shapes=[
            pltpu.VMEM(flat, BF16),
            pltpu.VMEM(flat, BF16),
            pltpu.VMEM((2, *flat[1:]), BF16),
            pltpu.VMEM((2, *flat[1:]), BF16),
            pltpu.VMEM((width, width), F32),
            pltpu.VMEM((width, width), F32),
            pltpu.VMEM((width, width), F32),
            pltpu.VMEM((width, width), F32),
            pltpu.VMEM((width, width), F32),
            pltpu.VMEM((4, width, width), F32),
            pltpu.VMEM((2, width, width), HALO),
            pltpu.VMEM((4, width, width), HALO),
            pltpu.VMEM((4, width, width), HALO),
            pltpu.VMEM((2, 1, width), F32),
            pltpu.VMEM((2, blocks, 1, width), F32),
            pltpu.VMEM((3, 1, width), F32),
            pltpu.VMEM((3, GRID, 1, width), F32),
            pltpu.VMEM((1, 2, width, width), BF16),
            pltpu.VMEM((1, 2, width, width), BF16),
            pltpu.VMEM((2, width, width), PART),
            pltpu.VMEM((2, width, width), PART),
            pltpu.VMEM((1, width), jnp.int32),
            pltpu.VMEM((1, width), jnp.int32),
            pltpu.VMEM((4, width, width), HALO),
            dma((count,)), dma((count,)), dma((count,)), dma, dma((4,)), dma((4,)),
            dma((2, 4)), dma((2, 4)), dma((2,)), dma((2,)), dma((3,)), dma((3,)),
            dma, dma((count // 2,)), dma((count // 2,)), dma((2,)), dma((2,)), dma((2,)), dma((2,)),
            dma((2,)), dma((4,)), dma((4,)),
        ],
        compiler_params=pltpu.CompilerParams(
            collective_id=0, has_side_effects=True, vmem_limit_bytes=60 * 1024 * 1024
        ),
        name="window",
    )(
        initial_state[0, 0],
        left_env.reshape(flat),
        edge_env.reshape(flat),
        right_env.reshape(flat),
        source_blocks,
        live_terms,
    )
    return state[None, None], energy


def solution(mesh):
    placed = (
        P("site", "sector", None, None),
        P("site", "sector", None, None, None, None),
        P("sector", None, None, None, None),
        P("site", "sector", None, None, None, None),
        P("site", "sector", None),
        P("site", "sector"),
    )
    return jax.shard_map(
        per_device,
        mesh=mesh,
        in_specs=placed,
        out_specs=(P("site", "sector", None, None), P("site")),
        check_vma=False,
    )
```
